512 devices in a mesh: comm: 8 (over y, core), node: 64 (over z, x).
Axes of the slice: x: 4, y: 4, z: 16, core: 2. Of those that a mesh axis runs over, the one named last changes fastest.
Arguments:
- embeddings: float32 [131072, 128], P('node'), may hold values from -1.2 to 75
- prototypes: float32 [4096, 128], P('comm'), may hold values from -3.6 to 3.6
- plan_grad: bfloat16 [131072, 4096], P('node', 'comm'), may hold values from -3 to 3
Outputs:
- grad_emb: float32 [131072, 128], P(('node', 'comm'))
- grad_proto: float32 [4096, 128], P(('comm', 'node'))
The draws below stay inside these ranges and needn't reach their ends.
All inputs are finite; a program needn't handle non-finite values.
Results may differ from the reference program's by a relative error of at most 0.0022.
Values sent between devices are 32-bit elements; how exact they have to be, the bound alone decides.
No kernel may reach another device: no remote copies, remote signals or barrier semaphores. Data moves between devices by JAX's collectives and lax.ppermute only.
A program may use at most 64 MiB of HBM per device.

```python
import math
import jax
import jax.numpy as jnp
from jax import lax

WIDTH = 128
PROTOS = 4096
NODES = 131072


def draw_embeddings(key, part):
    key = jax.random.fold_in(key, 11)
    key_scale, key_body = jax.random.split(key, 2)
    scales = jnp.exp(jax.random.uniform(key_scale, (NODES, 1), jnp.float32, math.log(0.3), math.log(3.0)))
    values = 0.06 * scales * jnp.clip(jax.random.normal(key_body, (NODES, WIDTH), jnp.float32), -6.0, 6.0)
    return values.astype(jnp.float32)


def draw_prototypes(key, part):
    key = jax.random.fold_in(key, 23)
    key_scale, key_body = jax.random.split(key, 2)
    scales = jnp.exp(jax.random.uniform(key_scale, (PROTOS, 1), jnp.float32, math.log(0.3), math.log(3.0)))
    values = 0.2 * scales * jnp.clip(jax.random.normal(key_body, (PROTOS, WIDTH), jnp.float32), -6.0, 6.0)
    return values.astype(jnp.float32)


def levels(own_key, shape, cuts, smallest, high):
    factor_of = 1.0
    for dim, blocks in cuts:
        heights = jax.random.uniform(jax.random.fold_in(jax.random.fold_in(own_key, 6), dim), (blocks,), jnp.float32, smallest / len(cuts), high / len(cuts))
        factor_of = factor_of * jnp.repeat(jnp.exp(heights), shape[dim] // blocks).reshape((-1,) + (1,) * (len(shape) - 1 - dim))
    return factor_of


def scatter_about(own_key, dims, scale, bound, shards=(), held_as=jnp.bfloat16):
    gain = levels(own_key, dims, shards, -0.22, 0.18) if shards else 1.0
    array = jax.random.normal(own_key, dims, jnp.float32) * scale * gain
    return jnp.minimum(jnp.maximum(array, -bound), bound).astype(held_as)


def setup_inputs(seed: int = 0) -> dict:
    arg_keys = jax.random.split(jax.random.key(seed), 4)
    embeddings = draw_embeddings(jax.random.fold_in(arg_keys[3], 71), 0)
    prototypes = draw_prototypes(jax.random.fold_in(arg_keys[3], 71), 0)
    plan_grad = scatter_about(arg_keys[2], (NODES, PROTOS), 0.5, 3.0, ((0, 64), (1, 8)))
    return {"embeddings": embeddings, "prototypes": prototypes, "plan_grad": plan_grad}


INV_EPS = 20.0


def reference(embeddings, prototypes, plan_grad):
    nodes = embeddings.shape[0]
    protos = prototypes.shape[0]
    width = embeddings.shape[1]
    log_mass = math.log(nodes / protos)
    factor = protos / nodes
    block = math.gcd(nodes, 2048)
    count = nodes // block
    emb_blocks = embeddings.reshape(count, block, width)
    grad_blocks = plan_grad.reshape(count, block, protos)

    def scores(rows_blk):
        return jnp.dot(rows_blk, prototypes.T, precision=lax.Precision.HIGHEST, preferred_element_type=jnp.float32) * INV_EPS

    def sweep(shift):
        def step(carry, rows_blk):
            col_max, col_sum = carry
            logits = scores(rows_blk)
            shifted = logits + shift[None, :]
            peak = jnp.max(shifted, axis=1)
            row_pot = -(peak + jnp.log(jnp.sum(jnp.exp(shifted - peak[:, None]), axis=1)))
            moved = logits + row_pot[:, None]
            top = jnp.maximum(col_max, jnp.max(moved, axis=0))
            col_sum = col_sum * jnp.exp(col_max - top) + jnp.sum(jnp.exp(moved - top[None, :]), axis=0)
            return (top, col_sum), row_pot

        start = (jnp.full((protos,), -jnp.inf, jnp.float32), jnp.zeros((protos,), jnp.float32))
        (top, total), row_pot = lax.scan(step, start, emb_blocks)
        return row_pot, log_mass - (top + jnp.log(total))

    f1, g1 = sweep(jnp.zeros((protos,), jnp.float32))
    f2, g2 = sweep(g1)

    def pass_one(acc, inputs):
        rows_blk, grad_blk, f2_blk = inputs
        logits = scores(rows_blk)
        plan = jnp.exp((logits + f2_blk[:, None]) + g2[None, :])
        weighted = grad_blk.astype(jnp.float32) * plan
        return acc + jnp.sum(weighted, axis=0), None

    dg2, _ = lax.scan(pass_one, jnp.zeros((protos,), jnp.float32), (emb_blocks, grad_blocks, f2))

    def pass_two(acc, inputs):
        rows_blk, grad_blk, f2_blk = inputs
        logits = scores(rows_blk)
        plan = jnp.exp((logits + f2_blk[:, None]) + g2[None, :])
        weighted = grad_blk.astype(jnp.float32) * plan
        df2 = jnp.sum(weighted, axis=1) - factor * jnp.sum(plan * dg2[None, :], axis=1)
        second = jnp.exp((logits + f2_blk[:, None]) + g1[None, :])
        return acc - jnp.sum(second * df2[:, None], axis=0), df2

    dg1, df2_all = lax.scan(pass_two, jnp.zeros((protos,), jnp.float32), (emb_blocks, grad_blocks, f2))

    def pass_three(acc, inputs):
        rows_blk, grad_blk, f1_blk, f2_blk, df2 = inputs
        logits = scores(rows_blk)
        plan = jnp.exp((logits + f2_blk[:, None]) + g2[None, :])
        weighted = grad_blk.astype(jnp.float32) * plan
        second = jnp.exp((logits + f2_blk[:, None]) + g1[None, :])
        first = jnp.exp(logits + f1_blk[:, None])
        scaled = jnp.exp((logits + f1_blk[:, None]) + (g1 - log_mass)[None, :])
        df1 = -jnp.sum(scaled * dg1[None, :], axis=1)
        dlog = weighted - factor * plan * dg2[None, :] - second * df2[:, None] - scaled * dg1[None, :] - first * df1[:, None]
        dscore = INV_EPS * dlog
        emb_out = jnp.dot(dscore, prototypes, precision=lax.Precision.HIGHEST, preferred_element_type=jnp.float32)
        proto_term = lax.dot_general(dscore, rows_blk, (((0,), (0,)), ((), ())), precision=lax.Precision.HIGHEST, preferred_element_type=jnp.float32)
        return acc + proto_term, emb_out

    grad_proto, grad_emb = lax.scan(pass_three, jnp.zeros((protos, width), jnp.float32), (emb_blocks, grad_blocks, f1, f2, df2_all))
    return grad_emb.reshape(nodes, width), grad_proto
```

```python
import math

import jax
import jax.numpy as jnp
from jax import lax
from jax.sharding import PartitionSpec as P

INV_EPS = 20.0


def to_all(values, axis):
    count = lax.axis_size(axis)
    copies = jnp.broadcast_to(values[None], (count,) + values.shape)
    return lax.all_to_all(copies, axis, 0, 0, tiled=True)


def merge(parts):
    peak = jnp.max(parts, axis=0)
    share = jnp.exp(parts - peak[None])
    mass = jnp.sum(share, axis=0)
    return peak + jnp.log(mass), share / mass[None]


def row_lse(shifted):
    peak = jnp.max(shifted, axis=1)
    mass = jnp.sum(jnp.exp(shifted - peak[:, None]), axis=1)
    return merge(to_all(peak + jnp.log(mass), "comm"))[0]


def scatter_sum(terms, axis):
    count = lax.axis_size(axis)
    blocks = terms.reshape(count, terms.shape[0] // count, terms.shape[1])
    return jnp.sum(lax.all_to_all(blocks, axis, 0, 0, tiled=True), axis=0)


def on_device(embeddings, prototypes, plan_grad):
    rows = embeddings.shape[0]
    local = prototypes.shape[0]
    comm_count = lax.axis_size("comm")
    node_count = lax.axis_size("node")
    per_proto = (rows * node_count) / (local * comm_count)
    log_mass = math.log(per_proto)
    factor = 1.0 / per_proto
    grads = plan_grad.astype(jnp.float32)
    logits = (
        jnp.dot(
            embeddings,
            prototypes.T,
            precision=lax.Precision.HIGHEST,
            preferred_element_type=jnp.float32,
        )
        * INV_EPS
    )
    f1 = -row_lse(logits)
    moved = logits + f1[:, None]
    peak = jnp.max(moved, axis=0)
    mass = jnp.sum(jnp.exp(moved - peak[None, :]), axis=0)
    g1 = log_mass - merge(to_all(peak + jnp.log(mass), "node"))[0]
    f2 = -row_lse(logits + g1[None, :])
    moved = logits + f2[:, None]
    peak = jnp.max(moved, axis=0)
    terms = jnp.exp(moved - peak[None, :])
    mass = jnp.sum(terms, axis=0)
    mean = jnp.sum(grads * terms, axis=0) / mass
    both = to_all(jnp.stack([peak + jnp.log(mass), mean]), "node")
    total, share = merge(both[:, 0])
    g2 = log_mass - total
    dg2 = per_proto * jnp.sum(share * both[:, 1], axis=0)
    plan = jnp.exp(logits + f2[:, None] + g2[None, :])
    df2 = jnp.sum(plan * (grads - factor * dg2[None, :]), axis=1)
    df2 = jnp.sum(to_all(df2, "comm"), axis=0)
    second = jnp.exp(logits + f2[:, None] + g1[None, :])
    dg1 = -jnp.sum(to_all(jnp.sum(second * df2[:, None], axis=0), "node"), axis=0)
    scaled = jnp.exp(logits + f1[:, None] + (g1 - log_mass)[None, :])
    df1 = -jnp.sum(to_all(jnp.sum(scaled * dg1[None, :], axis=1), "comm"), axis=0)
    first = jnp.exp(logits + f1[:, None])
    dscore = INV_EPS * (
        plan * (grads - factor * dg2[None, :])
        - second * df2[:, None]
        - scaled * dg1[None, :]
        - first * df1[:, None]
    )
    grad_proto = lax.dot_general(
        dscore,
        embeddings,
        (((0,), (0,)), ((), ())),
        precision=lax.Precision.HIGHEST,
        preferred_element_type=jnp.float32,
    )
    grad_emb = jnp.dot(
        dscore, prototypes, precision=lax.Precision.HIGHEST, preferred_element_type=jnp.float32
    )
    return scatter_sum(grad_emb, "comm"), scatter_sum(grad_proto, "node")


def solution(mesh):
    in_specs = (P("node", None), P("comm", None), P("node", "comm"))
    out_specs = (P(("node", "comm"), None), P(("comm", "node"), None))
    return jax.shard_map(
        on_device, mesh=mesh, in_specs=in_specs, out_specs=out_specs, check_vma=False
    )
```

```python
import math

import jax
import jax.numpy as jnp
from jax import lax
from jax.experimental import pallas as pl
from jax.experimental.pallas import tpu as pltpu
from jax.sharding import PartitionSpec as P

INV_EPS = 20.0
LOG2E = 1.0 / math.log(2.0)
LANES = 128
WIDE = 256
SPAN = 8
F32 = jnp.float32
BF16 = jnp.bfloat16
NT = (((1,), (1,)), ((), ()))
EVERY = slice(None)


def to_all(values, axis):
    count = lax.axis_size(axis)
    copies = jnp.broadcast_to(values[None], (count,) + values.shape)
    return lax.all_to_all(copies, axis, 0, 0, tiled=True)


def scatter_sum(terms, axis):
    count = lax.axis_size(axis)
    blocks = terms.reshape(count, terms.shape[0] // count, terms.shape[1])
    return jnp.sum(lax.all_to_all(blocks, axis, 0, 0, tiled=True), axis=0)


def split(x, pieces):
    out = []
    for _ in range(pieces):
        piece = x.astype(BF16)
        out.append(piece)
        x = x - piece.astype(F32)
    return out


def down(row):
    return jnp.transpose(jnp.broadcast_to(row, (LANES, row.shape[1])))


def tile_rows(at, tall):
    return pl.ds(pl.multiple_of(at * tall, tall), tall)


def lanes_of(ref, rows, tile):
    return ref[rows, tile * LANES : (tile + 1) * LANES]


def add_parts(parts):
    values = [parts[k] for k in range(parts.shape[0])]
    while len(values) > 1:
        values = [a + b for a, b in zip(values[::2], values[1::2])]
    return values[0]


def merge_parts(parts):
    count = parts.shape[0]
    peak = parts[0, 0:1, :]
    for k in range(1, count):
        peak = jnp.maximum(peak, parts[k, 0:1, :])
    mass = jnp.zeros(peak.shape, F32)
    mean = jnp.zeros(peak.shape, F32)
    for k in range(count):
        share = jnp.exp2(parts[k, 0:1, :] - peak)
        mass = mass + share
        if parts.shape[1] == 2:
            mean = mean + share * parts[k, 1:2, :]
    total = peak + jnp.log2(mass)
    return total if parts.shape[1] == 1 else (total, mean / mass)


def scores_kernel(emb, proto, grads, logits, turned, row_out, e_in, p_in, g_in, sems):
    chunks = 4
    size = emb.shape[0] // chunks
    get_p = pltpu.make_async_copy(proto, p_in, sems.at[0])
    get_p.start()
    get_e = []
    for k in range(chunks):
        rows = pl.ds(k * size, size)
        get_e.append(pltpu.make_async_copy(emb.at[rows], e_in.at[rows], sems.at[1 + k]))
        get_e[k].start()
    get_g = pltpu.make_async_copy(grads, g_in, sems.at[1 + chunks])
    get_g.start()
    get_p.wait()
    hi, mid, low = split(p_in[...] * (INV_EPS * LOG2E), 3)
    left = jnp.concatenate([hi, hi, hi, mid, mid, low], axis=1)
    for at in range(0, emb.shape[0], WIDE):
        if at % size == 0:
            get_e[at // size].wait()
        hi, mid, low = split(e_in[at : at + WIDE, :], 3)
        right = jnp.concatenate([hi, mid, low, hi, mid, hi], axis=1)
        tile = lax.dot_general(left, right, NT, preferred_element_type=F32)
        logits[:, at : at + WIDE] = tile
        peak = jnp.max(tile, axis=0, keepdims=True)
        mass = jnp.sum(jnp.exp2(tile - peak), axis=0, keepdims=True)
        row_out[:, at : at + WIDE] = peak + jnp.log2(mass)
    eye = (
        lax.broadcasted_iota(jnp.int32, (WIDE, WIDE), 0)
        == lax.broadcasted_iota(jnp.int32, (WIDE, WIDE), 1)
    ).astype(F32).astype(BF16)
    get_g.wait()
    for at in range(0, grads.shape[1], WIDE):
        turned[at : at + WIDE, :] = lax.dot_general(
            eye, g_in[:, at : at + WIDE], NT, preferred_element_type=F32
        ).astype(BF16)


def col_kernel(logits, parts, f1, lse_out, shifts, peaks, masses):
    tiles = logits.shape[1] // LANES
    f1[...] = -merge_parts(parts)
    shifts[...] = jnp.broadcast_to(f1[...], shifts.shape)

    def step(at, _):
        rows = tile_rows(at, 8)
        moved = [lanes_of(logits, rows, k) + lanes_of(shifts, EVERY, k) for k in range(tiles)]
        peak = moved[0]
        for part in moved[1:]:
            peak = jnp.maximum(peak, part)
        mass = jnp.exp2(moved[0] - peak)
        for part in moved[1:]:
            mass = mass + jnp.exp2(part - peak)
        peaks[rows, :] = peak
        masses[rows, :] = mass
        return 0

    lax.fori_loop(0, logits.shape[0] // 8, step, 0, unroll=4)
    peak_t = jnp.transpose(peaks[...])
    peak = jnp.max(peak_t, axis=0, keepdims=True)
    mass = jnp.sum(jnp.transpose(masses[...]) * jnp.exp2(peak_t - peak), axis=0, keepdims=True)
    lse_out[...] = peak + jnp.log2(mass)


def col_mean_kernel(logits, parts, grads, f2, out, shifts, peaks, masses, means):
    tiles = logits.shape[1] // LANES
    f2[...] = -merge_parts(parts)
    shifts[...] = jnp.broadcast_to(f2[...], shifts.shape)

    def step(at, _):
        rows = tile_rows(at, 16)
        peak = lanes_of(logits, rows, 0) + lanes_of(shifts, EVERY, 0)
        for k in range(1, tiles):
            peak = jnp.maximum(peak, lanes_of(logits, rows, k) + lanes_of(shifts, EVERY, k))
        mass = jnp.zeros((16, LANES), F32)
        mean = jnp.zeros((16, LANES), F32)
        for k in range(tiles):
            term = jnp.exp2(lanes_of(logits, rows, k) + lanes_of(shifts, EVERY, k) - peak)
            mass = mass + term
            mean = mean + term * lanes_of(grads, rows, k).astype(F32)
        peaks[rows, :] = peak
        masses[rows, :] = mass
        means[rows, :] = mean
        return 0

    lax.fori_loop(0, logits.shape[0] // 16, step, 0, unroll=2)
    peak_t = jnp.transpose(peaks[...])
    peak = jnp.max(peak_t, axis=0, keepdims=True)
    share = jnp.exp2(peak_t - peak)
    mass = jnp.sum(jnp.transpose(masses[...]) * share, axis=0, keepdims=True)
    mean = jnp.sum(jnp.transpose(means[...]) * share, axis=0, keepdims=True)
    out[0:1, :] = peak + jnp.log2(mass)
    out[1:2, :] = mean / mass


def span_lanes(span, tile):
    start = pl.multiple_of(span * (SPAN * LANES), SPAN * LANES)
    return pl.ds(start + tile * LANES, LANES)


def row_kernel(log_mass, logits, parts, g1, lse_out, shifts):
    g1[...] = log_mass - merge_parts(parts)
    shifts[...] = down(g1[...])
    count = logits.shape[0] // 8

    def over(span, _):
        lanes = [span_lanes(span, k) for k in range(SPAN)]

        def highest(at, peak):
            rows = tile_rows(at, 8)
            move = shifts[rows, :]
            return [jnp.maximum(peak[k], logits[rows, lanes[k]] + move) for k in range(SPAN)]

        peak = lax.fori_loop(
            0, count, highest, [jnp.full((8, LANES), -jnp.inf, F32)] * SPAN, unroll=16
        )
        peak = [jnp.max(part, axis=0, keepdims=True) for part in peak]

        def add(at, mass):
            rows = tile_rows(at, 8)
            move = shifts[rows, :]
            return [
                mass[k] + jnp.exp2(logits[rows, lanes[k]] + move - peak[k]) for k in range(SPAN)
            ]

        mass = lax.fori_loop(0, count, add, [jnp.zeros((8, LANES), F32)] * SPAN, unroll=16)
        for k in range(SPAN):
            total = jnp.sum(mass[k], axis=0, keepdims=True)
            lse_out[:, lanes[k]] = peak[k] + jnp.log2(total)
        return 0

    lax.fori_loop(0, logits.shape[1] // (SPAN * LANES), over, 0)


def df2_kernel(log_mass, factor, logits, f2, parts, grads, score, out, cols, weights):
    total, mean = merge_parts(parts)
    cols[...] = down(log_mass - total)
    weights[...] = down(mean)
    tall = 16

    def over(span, _):
        lanes = [span_lanes(span, k) for k in range(SPAN)]
        moves = [f2[:, s] for s in lanes]

        def add(at, total):
            rows = tile_rows(at, tall)
            move = cols[rows, :]
            weigh = weights[rows, :]
            new = []
            for k in range(SPAN):
                term = jnp.exp2(logits[rows, lanes[k]] + move + moves[k])
                term = term * (grads[rows, lanes[k]].astype(F32) - weigh)
                score[rows, lanes[k]] = term
                new.append(total[k] + term[:8] + term[8:])
            return new

        total = lax.fori_loop(
            0, logits.shape[0] // tall, add, [jnp.zeros((8, LANES), F32)] * SPAN, unroll=4
        )
        for k in range(SPAN):
            out[:, lanes[k]] = jnp.sum(total[k], axis=0, keepdims=True)
        return 0

    lax.fori_loop(0, logits.shape[1] // (SPAN * LANES), over, 0)


def dg1_kernel(logits, f2, g1, parts, score, rest, out, rows_of, weights, cols, sums):
    tiles = logits.shape[1] // LANES
    rows_of[...] = jnp.broadcast_to(f2[...], rows_of.shape)
    weights[...] = jnp.broadcast_to(add_parts(parts), weights.shape)
    cols[...] = down(g1[...])

    def step(at, _):
        rows = tile_rows(at, 8)
        move = cols[rows, :]
        total = jnp.zeros((8, LANES), F32)
        for k in range(tiles):
            term = jnp.exp2(lanes_of(logits, rows, k) + lanes_of(rows_of, EVERY, k) + move)
            term = term * lanes_of(weights, EVERY, k)
            rest[rows, k * LANES : (k + 1) * LANES] = lanes_of(score, rows, k) - term
            total = total + term
        sums[rows, :] = total
        return 0

    lax.fori_loop(0, logits.shape[0] // 8, step, 0, unroll=4)
    out[...] = -jnp.sum(jnp.transpose(sums[...]), axis=0, keepdims=True)


def df1_kernel(log_mass, logits, f1, g1, parts, score, rest, out, cols, weights):
    cols[...] = down(g1[...] - log_mass)
    weights[...] = down(add_parts(parts))
    tall = 8

    def over(span, _):
        lanes = [span_lanes(span, k) for k in range(SPAN)]
        moves = [f1[:, s] for s in lanes]

        def add(at, total):
            rows = tile_rows(at, tall)
            move = cols[rows, :]
            weigh = weights[rows, :]
            new = []
            for k in range(SPAN):
                term = jnp.exp2(logits[rows, lanes[k]] + move + moves[k]) * weigh
                rest[rows, lanes[k]] = score[rows, lanes[k]] - term
                new.append(total[k] + term)
            return new

        total = lax.fori_loop(
            0, logits.shape[0] // tall, add, [jnp.zeros((tall, LANES), F32)] * SPAN, unroll=8
        )
        for k in range(SPAN):
            out[:, lanes[k]] = -jnp.sum(total[k], axis=0, keepdims=True)
        return 0

    lax.fori_loop(0, logits.shape[1] // (SPAN * LANES), over, 0)


def grads_kernel(logits, f1, parts, score, proto, emb, emb_out, proto_out, df1, work):
    width = proto.shape[1]
    df1[...] = add_parts(parts)
    p_hi, p_low = split(jnp.transpose(proto[...]) * INV_EPS, 2)
    p_both = jnp.concatenate([p_hi, p_low], axis=0)
    proto_out[...] = jnp.zeros(proto_out.shape, F32)

    def tile(at, _):
        start = pl.multiple_of(at * WIDE, WIDE)
        parts = range(WIDE // LANES)
        lanes = [pl.ds(start + k * LANES, LANES) for k in parts]
        moves = [f1[:, s] for s in lanes]
        weights = [df1[:, s] for s in lanes]

        def fill(group, _):
            rows = tile_rows(group, 8)
            for k in parts:
                first = jnp.exp2(logits[rows, lanes[k]] + moves[k])
                work[rows, k * LANES : (k + 1) * LANES] = (
                    score[rows, lanes[k]] - first * weights[k]
                )
            return 0

        lax.fori_loop(0, logits.shape[0] // 8, fill, 0, unroll=16)
        s_hi, s_low = split(work[...], 2)
        both = jnp.dot(p_both, s_hi, preferred_element_type=F32)
        emb_out[:, pl.ds(start, WIDE)] = (
            both[:width] + both[width:] + jnp.dot(p_hi, s_low, preferred_element_type=F32)
        )
        e_hi, e_low = split(emb[pl.ds(start, WIDE), :] * INV_EPS, 2)
        both = jnp.dot(s_hi, jnp.concatenate([e_hi, e_low], axis=1), preferred_element_type=F32)
        proto_out[...] += (
            both[:, :width] + both[:, width:] + jnp.dot(s_low, e_hi, preferred_element_type=F32)
        )
        return 0

    lax.fori_loop(0, logits.shape[1] // WIDE, tile, 0)


def call(kernel, name, outs, scratch, args, places=None):
    vmem = pl.BlockSpec(memory_space=pltpu.VMEM)
    return pl.pallas_call(
        kernel,
        name=name,
        out_shape=[jax.ShapeDtypeStruct(shape, dtype) for shape, dtype in outs],
        in_specs=places or [vmem] * len(args),
        out_specs=[vmem] * len(outs),
        scratch_shapes=[
            s if not isinstance(s, tuple) else pltpu.VMEM(s, F32) for s in scratch
        ],
        compiler_params=pltpu.CompilerParams(vmem_limit_bytes=24 * 2**20),
    )(*args)


def on_device(embeddings, prototypes, plan_grad):
    rows, width = embeddings.shape
    local = prototypes.shape[0]
    per_proto = (rows * lax.axis_size("node")) / (local * lax.axis_size("comm"))
    log_mass = math.log2(per_proto)
    factor = 1.0 / per_proto
    full = ((local, rows), F32)
    row = ((1, rows), F32)
    col = ((1, local), F32)
    tall = (local, LANES)
    hbm = pl.BlockSpec(memory_space=pltpu.HBM)

    logits, grads, here = call(
        scores_kernel, "scores", [full, ((local, rows), BF16), row],
        [(rows, width), (local, width), pltpu.VMEM((rows, local), BF16),
         pltpu.SemaphoreType.DMA((6,))],
        [embeddings, prototypes, plan_grad], [hbm] * 3,
    )
    f1, here = call(
        col_kernel, "col_lse", [row, col], [(8, rows), tall, tall],
        [logits, to_all(here, "comm")],
    )
    g1, here = call(
        lambda *refs: row_kernel(log_mass, *refs), "row_lse", [col, row], [tall],
        [logits, to_all(here, "node")],
    )
    f2, here = call(
        col_mean_kernel, "col_lse_mean", [row, ((2, local), F32)],
        [(16, rows), tall, tall, tall], [logits, to_all(here, "comm"), grads],
    )
    score, here = call(
        lambda *refs: df2_kernel(log_mass, factor, *refs), "df2", [full, row], [tall, tall],
        [logits, f2, to_all(here, "node"), grads],
    )
    score, here = call(
        dg1_kernel, "dg1", [full, col], [(8, rows), (8, rows), tall, tall],
        [logits, f2, g1, to_all(here, "comm"), score],
    )
    score, here = call(
        lambda *refs: df1_kernel(log_mass, *refs), "df1", [full, row], [tall, tall],
        [logits, f1, g1, to_all(here, "node"), score],
    )
    emb_part, proto_part = call(
        grads_kernel, "grads", [((width, rows), F32), ((local, width), F32)],
        [(1, rows), (local, WIDE)],
        [logits, f1, to_all(here, "comm"), score, prototypes, embeddings],
    )
    grad_emb = lax.psum_scatter(emb_part.T, "comm", scatter_dimension=0, tiled=True)
    grad_proto = scatter_sum(proto_part, "node")
    return grad_emb, grad_proto


def solution(mesh):
    in_specs = (P("node", None), P("comm", None), P("node", "comm"))
    out_specs = (P(("node", "comm"), None), P(("comm", "node"), None))
    return jax.shard_map(
        on_device, mesh=mesh, in_specs=in_specs, out_specs=out_specs, check_vma=False
    )
```

```python
import math

import jax
import jax.numpy as jnp
from jax import lax
from jax.experimental import pallas as pl
from jax.experimental.pallas import tpu as pltpu
from jax.sharding import Mesh
from jax.sharding import PartitionSpec as P

INV_EPS = 20.0
LOG2E = 1.0 / math.log(2.0)
LANES = 128
WIDE = 256
SPAN = 4
F32 = jnp.float32
BF16 = jnp.bfloat16
NT = (((1,), (1,)), ((), ()))
EVERY = slice(None)


def to_all(values, axis):
    count = lax.axis_size(axis)
    copies = jnp.broadcast_to(values[None], (count,) + values.shape)
    return lax.all_to_all(copies, axis, 0, 0, tiled=True)


def scatter_sum(blocks, axis):
    return jnp.sum(lax.all_to_all(blocks, axis, 0, 0, tiled=True), axis=0)


def split(x, pieces):
    out = []
    for _ in range(pieces):
        piece = x.astype(BF16)
        out.append(piece)
        x = x - piece.astype(F32)
    return out


def times(left, right):
    hi, low = split(right, 2)
    both = jnp.dot(jnp.concatenate(left, axis=0), hi, preferred_element_type=F32)
    size = left[0].shape[0]
    return both[:size] + both[size:] + jnp.dot(left[0], low, preferred_element_type=F32)


def down(row):
    return jnp.transpose(jnp.broadcast_to(row, (LANES, row.shape[1])))


def tile_rows(at, tall):
    return pl.ds(pl.multiple_of(at * tall, tall), tall)


def lanes_of(ref, rows, tile):
    return ref[rows, tile * LANES : (tile + 1) * LANES]


def add_parts(parts):
    values = [parts[k] for k in range(parts.shape[0])]
    while len(values) > 1:
        values = [a + b for a, b in zip(values[::2], values[1::2])]
    return values[0]


def merge_parts(parts):
    count = parts.shape[0]
    peak = parts[0, 0:1, :]
    for k in range(1, count):
        peak = jnp.maximum(peak, parts[k, 0:1, :])
    mass = jnp.zeros(peak.shape, F32)
    mean = jnp.zeros(peak.shape, F32)
    for k in range(count):
        share = jnp.exp2(parts[k, 0:1, :] - peak)
        mass = mass + share
        if parts.shape[1] == 2:
            mean = mean + share * parts[k, 1:2, :]
    total = peak + jnp.log2(mass)
    return total if parts.shape[1] == 1 else (total, mean / mass)


def scores_kernel(
    emb, proto, grads,
    logits, turned, row_out, e_in, p_in, g_in, sems,
):
    chunks = 4
    size = emb.shape[0] // chunks
    get_p = pltpu.make_async_copy(proto, p_in, sems.at[0])
    get_p.start()
    get_e = []
    for k in range(chunks):
        rows = pl.ds(k * size, size)
        get_e.append(pltpu.make_async_copy(emb.at[rows], e_in.at[rows], sems.at[1 + k]))
        get_e[k].start()
    get_g = pltpu.make_async_copy(grads, g_in, sems.at[1 + chunks])
    get_g.start()
    get_p.wait()
    hi, mid, low = split(p_in[...] * (INV_EPS * LOG2E), 3)
    left = jnp.concatenate([hi, hi, hi, mid, mid, low], axis=1)
    for at in range(0, emb.shape[0], 2 * size):
        get_e[at // size].wait()
        get_e[at // size + 1].wait()
        lanes = slice(at, at + 2 * size)
        hi, mid, low = split(e_in[lanes, :], 3)
        right = jnp.concatenate([hi, mid, low, hi, mid, hi], axis=1)
        tile = lax.dot_general(left, right, NT, preferred_element_type=F32)
        logits[:, lanes] = tile
        peak = jnp.max(tile, axis=0, keepdims=True)
        mass = jnp.sum(jnp.exp2(tile - peak), axis=0, keepdims=True)
        row_out[:, lanes] = peak + jnp.log2(mass)
    eye = (
        lax.broadcasted_iota(jnp.int32, (WIDE, WIDE), 0)
        == lax.broadcasted_iota(jnp.int32, (WIDE, WIDE), 1)
    ).astype(F32).astype(BF16)
    get_g.wait()
    for at in range(0, grads.shape[1], WIDE):
        turned[at : at + WIDE, :] = lax.dot_general(
            eye, g_in[:, at : at + WIDE], NT, preferred_element_type=F32
        ).astype(BF16)


def col_kernel(logits, parts, f1, lse_out, shifts, peaks, masses):
    tiles = logits.shape[1] // LANES
    f1[...] = -merge_parts(parts)
    shifts[...] = jnp.broadcast_to(f1[...], shifts.shape)

    def step(at, _):
        rows = tile_rows(at, 8)
        moved = [lanes_of(logits, rows, k) + lanes_of(shifts, EVERY, k) for k in range(tiles)]
        peak = moved[0]
        for part in moved[1:]:
            peak = jnp.maximum(peak, part)
        mass = jnp.exp2(moved[0] - peak)
        for part in moved[1:]:
            mass = mass + jnp.exp2(part - peak)
        peaks[rows, :] = peak
        masses[rows, :] = mass
        return 0

    lax.fori_loop(0, logits.shape[0] // 8, step, 0, unroll=4)
    peak_t = jnp.transpose(peaks[...])
    peak = jnp.max(peak_t, axis=0, keepdims=True)
    mass = jnp.sum(jnp.transpose(masses[...]) * jnp.exp2(peak_t - peak), axis=0, keepdims=True)
    lse_out[...] = peak + jnp.log2(mass)


def merge_kernel(parts, out):
    total, mean = merge_parts(parts)
    out[0:1, :] = total
    out[1:2, :] = mean


def col_mean_kernel(logits, parts, grads, f2, out, shifts, peaks, masses, means):
    tiles = logits.shape[1] // LANES
    f2[...] = -merge_parts(parts)
    shifts[...] = jnp.broadcast_to(f2[...], shifts.shape)

    def step(at, _):
        rows = tile_rows(at, 16)
        peak = lanes_of(logits, rows, 0) + lanes_of(shifts, EVERY, 0)
        for k in range(1, tiles):
            peak = jnp.maximum(peak, lanes_of(logits, rows, k) + lanes_of(shifts, EVERY, k))
        mass = jnp.zeros((16, LANES), F32)
        mean = jnp.zeros((16, LANES), F32)
        for k in range(tiles):
            term = jnp.exp2(lanes_of(logits, rows, k) + lanes_of(shifts, EVERY, k) - peak)
            mass = mass + term
            mean = mean + term * lanes_of(grads, rows, k).astype(F32)
        peaks[rows, :] = peak
        masses[rows, :] = mass
        means[rows, :] = mean
        return 0

    lax.fori_loop(0, logits.shape[0] // 16, step, 0, unroll=2)
    peak_t = jnp.transpose(peaks[...])
    peak = jnp.max(peak_t, axis=0, keepdims=True)
    share = jnp.exp2(peak_t - peak)
    mass = jnp.sum(jnp.transpose(masses[...]) * share, axis=0, keepdims=True)
    mean = jnp.sum(jnp.transpose(means[...]) * share, axis=0, keepdims=True)
    out[0:1, :] = peak + jnp.log2(mass)
    out[1:2, :] = mean / mass


def spans(ref, size):
    tiles = ref.shape[1] // LANES
    for at in range(0, tiles, size):
        yield [slice(k * LANES, (k + 1) * LANES) for k in range(at, at + size)]


def row_kernel(log_mass, logits, parts, g1, lse_out, shifts):
    g1[...] = log_mass - merge_parts(parts)
    shifts[...] = down(g1[...])
    count = logits.shape[0] // 8
    for lanes in spans(logits, SPAN):

        def highest(at, peak):
            rows = tile_rows(at, 8)
            move = shifts[rows, :]
            return [jnp.maximum(p, logits[rows, s] + move) for p, s in zip(peak, lanes)]

        peak = lax.fori_loop(
            0, count, highest, [jnp.full((8, LANES), -jnp.inf, F32)] * SPAN, unroll=count
        )
        peak = [jnp.max(part, axis=0, keepdims=True) for part in peak]

        def add(at, mass):
            rows = tile_rows(at, 8)
            move = shifts[rows, :]
            return [
                m + jnp.exp2(logits[rows, s] + move - p) for m, p, s in zip(mass, peak, lanes)
            ]

        mass = lax.fori_loop(0, count, add, [jnp.zeros((8, LANES), F32)] * SPAN, unroll=count)
        for p, m, s in zip(peak, mass, lanes):
            lse_out[:, s] = p + jnp.log2(jnp.sum(m, axis=0, keepdims=True))


def df2_kernel(log_mass, logits, f2, parts, grads, score, out, cols, weights):
    total, mean = merge_parts(parts)
    cols[...] = down(log_mass - total)
    weights[...] = down(mean)
    tall = 16
    count = logits.shape[0] // tall
    for lanes in spans(logits, SPAN):
        moves = [f2[:, s] for s in lanes]

        def add(at, total):
            rows = tile_rows(at, tall)
            move = cols[rows, :]
            weigh = weights[rows, :]
            new = []
            for t, m, s in zip(total, moves, lanes):
                term = jnp.exp2(logits[rows, s] + move + m)
                term = term * (grads[rows, s].astype(F32) - weigh)
                score[rows, s] = term
                new.append(t + term[:8] + term[8:])
            return new

        total = lax.fori_loop(0, count, add, [jnp.zeros((8, LANES), F32)] * SPAN, unroll=count)
        for t, s in zip(total, lanes):
            out[:, s] = jnp.sum(t, axis=0, keepdims=True)


def dg1_kernel(logits, f2, g1, parts, score, rest, out, rows_of, weights, cols, sums):
    tiles = logits.shape[1] // LANES
    rows_of[...] = jnp.broadcast_to(f2[...], rows_of.shape)
    weights[...] = jnp.broadcast_to(add_parts(parts), weights.shape)
    cols[...] = down(g1[...])

    def step(at, _):
        rows = tile_rows(at, 8)
        move = cols[rows, :]
        total = jnp.zeros((8, LANES), F32)
        for k in range(tiles):
            term = jnp.exp2(lanes_of(logits, rows, k) + lanes_of(rows_of, EVERY, k) + move)
            term = term * lanes_of(weights, EVERY, k)
            rest[rows, k * LANES : (k + 1) * LANES] = lanes_of(score, rows, k) - term
            total = total + term
        sums[rows, :] = total
        return 0

    lax.fori_loop(0, logits.shape[0] // 8, step, 0, unroll=4)
    out[...] = -jnp.sum(jnp.transpose(sums[...]), axis=0, keepdims=True)


def proto_term(score, emb):
    width = emb.shape[1]
    s_hi, s_low = split(score, 2)
    e_hi, e_low = split(emb * INV_EPS, 2)
    both = jnp.dot(s_hi, jnp.concatenate([e_hi, e_low], axis=1), preferred_element_type=F32)
    low = jnp.dot(s_low, e_hi, preferred_element_type=F32)
    return both[:, :width] + both[:, width:] + low


def df1_kernel(log_mass, logits, f1, g1, parts, score, rest, out, cols, weights):
    cols[...] = down(g1[...] - log_mass)
    weights[...] = down(add_parts(parts))
    count = logits.shape[0] // 8
    for lanes in spans(logits, SPAN):
        moves = [f1[:, s] for s in lanes]

        def add(at, total):
            rows = tile_rows(at, 8)
            move = cols[rows, :]
            weigh = weights[rows, :]
            new = []
            for t, m, s in zip(total, moves, lanes):
                term = jnp.exp2(logits[rows, s] + move + m) * weigh
                rest[rows, s] = score[rows, s] - term
                new.append(t + term)
            return new

        total = lax.fori_loop(0, count, add, [jnp.zeros((8, LANES), F32)] * SPAN, unroll=count)
        for t, s in zip(total, lanes):
            out[:, s] = -jnp.sum(t, axis=0, keepdims=True)


def proto_kernel(logits, f1, parts, score, emb, dlog, proto_out):
    df1 = add_parts(parts)
    step = 2 * SPAN * LANES
    total = jnp.zeros((logits.shape[0], emb.shape[1]), F32)
    for at in range(0, logits.shape[1], step):
        nodes = slice(at, at + step)
        dlog[:, nodes] = score[:, nodes] - jnp.exp2(logits[:, nodes] + f1[:, nodes]) * df1[:, nodes]
        total = total + proto_term(dlog[:, nodes], emb[nodes, :])
    xs, zs, tall, _ = proto_out.shape
    for x in range(xs):
        for z in range(zs):
            start = (z * xs + x) * tall
            proto_out[x, z] = total[start : start + tall]


def emb_kernel(place, dlog, proto, keep, send):
    turned_p = split(jnp.transpose(proto[...]) * INV_EPS, 2)
    size = keep.shape[2]
    part = times(turned_p, dlog[...])
    for y in range(keep.shape[0]):
        even = part[:, 2 * y * size : (2 * y + 1) * size]
        odd = part[:, (2 * y + 1) * size : (2 * y + 2) * size]

        @pl.when(place[1] == 0)
        def _():
            keep[y] = even
            send[y] = odd

        @pl.when(place[1] != 0)
        def _():
            keep[y] = odd
            send[y] = even


def pair_kernel(place, keep, other, *outs):
    for k, out in enumerate(outs):
        y = place[0] ^ k
        out[...] = keep[y] + other[y]


def last_kernel(*refs):
    *parts, out = refs
    total = parts[0][...]
    for part in parts[1:]:
        total = total + part[...]
    out[...] = jnp.transpose(total)


def call(kernel, name, outs, scratch, args, in_places=(), out_places=()):
    vmem = pl.BlockSpec(memory_space=pltpu.VMEM)
    place = lambda places, k: pl.BlockSpec(memory_space=places[k]) if k in places else vmem
    return pl.pallas_call(
        kernel,
        name=name,
        out_shape=[
            dict(out_places)[k](shape, dtype)
            if k in dict(out_places)
            else jax.ShapeDtypeStruct(shape, dtype)
            for k, (shape, dtype) in enumerate(outs)
        ],
        in_specs=[place(dict(in_places), k) for k in range(len(args))],
        out_specs=[place(dict(out_places), k) for k in range(len(outs))],
        scratch_shapes=[
            s if not isinstance(s, tuple) else pltpu.VMEM(s, F32) for s in scratch
        ],
        compiler_params=pltpu.CompilerParams(vmem_limit_bytes=24 * 2**20),
    )(*args)


def on_device(embeddings, prototypes, plan_grad):
    rows, width = embeddings.shape
    local = prototypes.shape[0]
    ys = lax.axis_size("y")
    comms = ys * lax.axis_size("core")
    xs = lax.axis_size("x")
    zs = lax.axis_size("z")
    per_proto = (rows * zs * xs) / (local * comms)
    log_mass = math.log2(per_proto)
    full = ((local, rows), F32)
    row = ((1, rows), F32)
    col = ((1, local), F32)
    two = ((2, local), F32)
    tall = (local, LANES)
    block = ((width, rows // comms), F32)
    blocks = ((ys,) + block[0], F32)
    node = ("z", "x")
    comm = ("y", "core")
    hbm = pltpu.HBM
    place = jnp.stack([lax.axis_index("y"), lax.axis_index("core")])

    logits, grads, here = call(
        scores_kernel, "scores", [full, ((local, rows), BF16), row],
        [(rows, width), (local, width), pltpu.VMEM((rows, local), BF16),
         pltpu.SemaphoreType.DMA((6,))],
        [pltpu.with_memory_space_constraint(x, hbm)
         for x in (embeddings, prototypes, plan_grad)],
        {0: hbm, 1: hbm, 2: hbm},
    )
    here, place = lax.optimization_barrier((here, place))
    f1, here = call(
        col_kernel, "col_lse", [row, col], [(8, rows), tall, tall], [logits, to_all(here, comm)]
    )
    g1, here = call(
        lambda *refs: row_kernel(log_mass, *refs), "row_lse", [col, row], [tall],
        [logits, to_all(here, node)],
    )
    f2, here = call(
        col_mean_kernel, "col_lse_mean", [row, two],
        [(16, rows), tall, tall, tall], [logits, to_all(here, comm), grads],
    )
    (here,) = call(merge_kernel, "merge_x", [two], [], [to_all(here, "x")])
    score, here = call(
        lambda *refs: df2_kernel(log_mass, *refs), "df2", [full, row], [tall, tall],
        [logits, f2, to_all(here, "z"), grads],
    )
    score, here = call(
        dg1_kernel, "dg1", [full, col], [(8, rows), (8, rows), tall, tall],
        [logits, f2, g1, to_all(here, comm), score],
    )
    score, here = call(
        lambda *refs: df1_kernel(log_mass, *refs), "df1", [full, row], [tall, tall],
        [logits, f1, g1, to_all(here, node), score],
    )
    dlog, proto_part = call(
        proto_kernel, "proto", [full, ((xs, zs, local // (xs * zs), width), F32)], [],
        [logits, f1, to_all(here, comm), score, embeddings],
    )
    grad_proto = scatter_sum(scatter_sum(proto_part, "x"), "z")
    keep, send = call(
        emb_kernel, "emb", [blocks, blocks], [], [place, dlog, prototypes], {0: pltpu.SMEM}
    )
    other = lax.ppermute(send, "core", [(0, 1), (1, 0)])
    parts = call(
        pair_kernel, "emb_pair", [block] * ys, [], [place, keep, other], {0: pltpu.SMEM}
    )
    parts = list(parts)
    for k in range(1, ys):
        parts[k] = lax.ppermute(parts[k], "y", [(y, y ^ k) for y in range(ys)])
    (grad_emb,) = call(last_kernel, "emb_last", [(block[0][::-1], F32)], [], parts)
    return grad_emb, grad_proto


def solution(mesh):
    split_mesh = Mesh(mesh.devices.reshape(4, 2, 16, 4), ("y", "core", "z", "x"))
    node = ("z", "x")
    comm = ("y", "core")
    in_specs = (P(node, None), P(comm, None), P(node, comm))
    out_specs = (P(node + comm, None), P(comm + node, None))
    return jax.shard_map(
        on_device, mesh=split_mesh, in_specs=in_specs, out_specs=out_specs, check_vma=False
    )
```

```python
import math

import jax
import jax.numpy as jnp
from jax import lax
from jax.experimental import pallas as pl
from jax.experimental.pallas import tpu as pltpu
from jax.sharding import Mesh
from jax.sharding import PartitionSpec as P

INV_EPS = 20.0
LOG2E = 1.0 / math.log(2.0)
LANES = 128
WIDE = 256
SPAN = 4
F32 = jnp.float32
BF16 = jnp.bfloat16
NT = (((1,), (1,)), ((), ()))
EVERY = slice(None)


def to_all(values, axis):
    count = lax.axis_size(axis)
    copies = jnp.broadcast_to(values[None], (count,) + values.shape)
    return lax.all_to_all(copies, axis, 0, 0, tiled=True)


def scatter_sum(blocks, axis):
    return jnp.sum(lax.all_to_all(blocks, axis, 0, 0, tiled=True), axis=0)


def split(x, pieces):
    out = []
    for _ in range(pieces):
        piece = x.astype(BF16)
        out.append(piece)
        x = x - piece.astype(F32)
    return out


def times(left, right):
    hi, low = split(right, 2)
    both = jnp.dot(jnp.concatenate(left, axis=0), hi, preferred_element_type=F32)
    size = left[0].shape[0]
    return both[:size] + both[size:] + jnp.dot(left[0], low, preferred_element_type=F32)


def down(row):
    return jnp.transpose(jnp.broadcast_to(row, (LANES, row.shape[1])))


def tile_rows(at, tall):
    return pl.ds(pl.multiple_of(at * tall, tall), tall)


def lanes_of(ref, rows, tile):
    return ref[rows, tile * LANES : (tile + 1) * LANES]


def add_parts(parts):
    values = [parts[k] for k in range(parts.shape[0])]
    while len(values) > 1:
        values = [a + b for a, b in zip(values[::2], values[1::2])]
    return values[0]


def merge_parts(parts):
    count = parts.shape[0]
    peak = parts[0, 0:1, :]
    for k in range(1, count):
        peak = jnp.maximum(peak, parts[k, 0:1, :])
    mass = jnp.zeros(peak.shape, F32)
    mean = jnp.zeros(peak.shape, F32)
    for k in range(count):
        share = jnp.exp2(parts[k, 0:1, :] - peak)
        mass = mass + share
        if parts.shape[1] == 2:
            mean = mean + share * parts[k, 1:2, :]
    total = peak + jnp.log2(mass)
    return total if parts.shape[1] == 1 else (total, mean / mass)


def scores_kernel(
    emb, proto, grads,
    logits, turned, row_out, e_in, p_in, g_in, sems,
):
    chunks = 4
    size = emb.shape[0] // chunks
    get_p = pltpu.make_async_copy(proto, p_in, sems.at[0])
    get_p.start()
    get_e = []
    for k in range(chunks):
        rows = pl.ds(k * size, size)
        get_e.append(pltpu.make_async_copy(emb.at[rows], e_in.at[rows], sems.at[1 + k]))
        get_e[k].start()
    get_g = pltpu.make_async_copy(grads, g_in, sems.at[1 + chunks])
    get_g.start()
    get_p.wait()
    hi, mid, low = split(p_in[...] * (INV_EPS * LOG2E), 3)
    left = jnp.concatenate([hi, hi, hi, mid, mid, low], axis=1)
    for get in get_e:
        get.wait()
    for at in range(0, emb.shape[0], size):
        lanes = slice(at, at + size)
        hi, mid, low = split(e_in[lanes, :], 3)
        right = jnp.concatenate([hi, mid, low, hi, mid, hi], axis=1)
        tile = lax.dot_general(left, right, NT, preferred_element_type=F32)
        logits[:, lanes] = tile
        if at + size == emb.shape[0]:
            get_g.wait()
        peak = jnp.max(tile, axis=0, keepdims=True)
        mass = jnp.sum(jnp.exp2(tile - peak), axis=0, keepdims=True)
        row_out[:, lanes] = peak + jnp.log2(mass)
    eye = (
        lax.broadcasted_iota(jnp.int32, (WIDE, WIDE), 0)
        == lax.broadcasted_iota(jnp.int32, (WIDE, WIDE), 1)
    ).astype(F32).astype(BF16)
    for at in range(0, grads.shape[1], WIDE):
        turned[at : at + WIDE, :] = lax.dot_general(
            eye, g_in[:, at : at + WIDE], NT, preferred_element_type=F32
        ).astype(BF16)


def col_kernel(logits, parts, f1, lse_out, shifts, peaks, masses):
    tiles = logits.shape[1] // LANES
    f1[...] = -merge_parts(parts)
    shifts[...] = jnp.broadcast_to(f1[...], shifts.shape)

    def step(at, _):
        rows = tile_rows(at, 8)
        moved = [lanes_of(logits, rows, k) + lanes_of(shifts, EVERY, k) for k in range(tiles)]
        peak = moved[0]
        for part in moved[1:]:
            peak = jnp.maximum(peak, part)
        mass = jnp.exp2(moved[0] - peak)
        for part in moved[1:]:
            mass = mass + jnp.exp2(part - peak)
        peaks[rows, :] = peak
        masses[rows, :] = mass
        return 0

    lax.fori_loop(0, logits.shape[0] // 8, step, 0, unroll=4)
    peak_t = jnp.transpose(peaks[...])
    peak = jnp.max(peak_t, axis=0, keepdims=True)
    mass = jnp.sum(jnp.transpose(masses[...]) * jnp.exp2(peak_t - peak), axis=0, keepdims=True)
    lse_out[...] = peak + jnp.log2(mass)


def merge_kernel(parts, out):
    total, mean = merge_parts(parts)
    out[0:1, :] = total
    out[1:2, :] = mean


def col_mean_kernel(logits, parts, grads, f2, out, shifts, peaks, masses, means):
    tiles = logits.shape[1] // LANES
    f2[...] = -merge_parts(parts)
    shifts[...] = jnp.broadcast_to(f2[...], shifts.shape)

    def step(at, _):
        rows = tile_rows(at, 16)
        peak = lanes_of(logits, rows, 0) + lanes_of(shifts, EVERY, 0)
        for k in range(1, tiles):
            peak = jnp.maximum(peak, lanes_of(logits, rows, k) + lanes_of(shifts, EVERY, k))
        mass = jnp.zeros((16, LANES), F32)
        mean = jnp.zeros((16, LANES), F32)
        for k in range(tiles):
            term = jnp.exp2(lanes_of(logits, rows, k) + lanes_of(shifts, EVERY, k) - peak)
            mass = mass + term
            mean = mean + term * lanes_of(grads, rows, k).astype(F32)
        peaks[rows, :] = peak
        masses[rows, :] = mass
        means[rows, :] = mean
        return 0

    lax.fori_loop(0, logits.shape[0] // 16, step, 0, unroll=2)
    peak_t = jnp.transpose(peaks[...])
    peak = jnp.max(peak_t, axis=0, keepdims=True)
    share = jnp.exp2(peak_t - peak)
    mass = jnp.sum(jnp.transpose(masses[...]) * share, axis=0, keepdims=True)
    mean = jnp.sum(jnp.transpose(means[...]) * share, axis=0, keepdims=True)
    out[0:1, :] = peak + jnp.log2(mass)
    out[1:2, :] = mean / mass


def spans(ref, size):
    tiles = ref.shape[1] // LANES
    for at in range(0, tiles, size):
        yield [slice(k * LANES, (k + 1) * LANES) for k in range(at, at + size)]


def row_kernel(log_mass, logits, parts, g1, lse_out, shifts):
    g1[...] = log_mass - merge_parts(parts)
    shifts[...] = down(g1[...])
    count = logits.shape[0] // 8
    for lanes in spans(logits, SPAN):

        def highest(at, peak):
            rows = tile_rows(at, 8)
            move = shifts[rows, :]
            return [jnp.maximum(p, logits[rows, s] + move) for p, s in zip(peak, lanes)]

        peak = lax.fori_loop(
            0, count, highest, [jnp.full((8, LANES), -jnp.inf, F32)] * SPAN, unroll=count
        )
        peak = [jnp.max(part, axis=0, keepdims=True) for part in peak]

        def add(at, mass):
            rows = tile_rows(at, 8)
            move = shifts[rows, :]
            return [
                m + jnp.exp2(logits[rows, s] + move - p) for m, p, s in zip(mass, peak, lanes)
            ]

        mass = lax.fori_loop(0, count, add, [jnp.zeros((8, LANES), F32)] * SPAN, unroll=count)
        for p, m, s in zip(peak, mass, lanes):
            lse_out[:, s] = p + jnp.log2(jnp.sum(m, axis=0, keepdims=True))


def df2_kernel(log_mass, logits, f2, parts, grads, score, out, cols, weights):
    total, mean = merge_parts(parts)
    cols[...] = down(log_mass - total)
    weights[...] = down(mean)
    tall = 16
    count = logits.shape[0] // tall
    for lanes in spans(logits, SPAN):
        moves = [f2[:, s] for s in lanes]

        def add(at, total):
            rows = tile_rows(at, tall)
            move = cols[rows, :]
            weigh = weights[rows, :]
            new = []
            for t, m, s in zip(total, moves, lanes):
                term = jnp.exp2(logits[rows, s] + move + m)
                term = term * (grads[rows, s].astype(F32) - weigh)
                score[rows, s] = term
                new.append(t + term[:8] + term[8:])
            return new

        total = lax.fori_loop(0, count, add, [jnp.zeros((8, LANES), F32)] * SPAN, unroll=count)
        for t, s in zip(total, lanes):
            out[:, s] = jnp.sum(t, axis=0, keepdims=True)


def dg1_kernel(logits, f2, g1, parts, score, rest, out, rows_of, weights, cols, sums):
    tiles = logits.shape[1] // LANES
    rows_of[...] = jnp.broadcast_to(f2[...], rows_of.shape)
    weights[...] = jnp.broadcast_to(add_parts(parts), weights.shape)
    cols[...] = down(g1[...])

    def step(at, _):
        rows = tile_rows(at, 8)
        move = cols[rows, :]
        total = jnp.zeros((8, LANES), F32)
        for k in range(tiles):
            term = jnp.exp2(lanes_of(logits, rows, k) + lanes_of(rows_of, EVERY, k) + move)
            term = term * lanes_of(weights, EVERY, k)
            rest[rows, k * LANES : (k + 1) * LANES] = lanes_of(score, rows, k) - term
            total = total + term
        sums[rows, :] = total
        return 0

    lax.fori_loop(0, logits.shape[0] // 8, step, 0, unroll=4)
    out[...] = -jnp.sum(jnp.transpose(sums[...]), axis=0, keepdims=True)


def proto_term(score, emb):
    width = emb.shape[1]
    s_hi, s_low = split(score, 2)
    e_hi, e_low = split(emb * INV_EPS, 2)
    both = jnp.dot(s_hi, jnp.concatenate([e_hi, e_low], axis=1), preferred_element_type=F32)
    low = jnp.dot(s_low, e_hi, preferred_element_type=F32)
    return both[:, :width] + both[:, width:] + low


def df1_kernel(log_mass, logits, f1, g1, parts, score, rest, out, cols, weights):
    cols[...] = down(g1[...] - log_mass)
    weights[...] = down(add_parts(parts))
    count = logits.shape[0] // 8
    for lanes in spans(logits, SPAN):
        moves = [f1[:, s] for s in lanes]

        def add(at, total):
            rows = tile_rows(at, 8)
            move = cols[rows, :]
            weigh = weights[rows, :]
            new = []
            for t, m, s in zip(total, moves, lanes):
                term = jnp.exp2(logits[rows, s] + move + m) * weigh
                rest[rows, s] = score[rows, s] - term
                new.append(t + term)
            return new

        total = lax.fori_loop(0, count, add, [jnp.zeros((8, LANES), F32)] * SPAN, unroll=count)
        for t, s in zip(total, lanes):
            out[:, s] = -jnp.sum(t, axis=0, keepdims=True)


def grads_kernel(place, logits, f1, parts, score, emb, proto, keep, send, proto_out):
    df1 = add_parts(parts)
    turned_p = split(jnp.transpose(proto[...]) * INV_EPS, 2)
    size = keep.shape[2]
    step = 4 * size
    total = jnp.zeros(proto_out.shape, F32)
    for at in range(0, logits.shape[1], step):
        nodes = slice(at, at + step)
        dlog = score[:, nodes] - jnp.exp2(logits[:, nodes] + f1[:, nodes]) * df1[:, nodes]
        part = times(turned_p, dlog)
        for k in range(0, step // size, 2):
            y = (at // size + k) // 2
            even = part[:, k * size : (k + 1) * size]
            odd = part[:, (k + 1) * size : (k + 2) * size]
            first = place[1] == 0
            keep[y] = jnp.where(first, even, odd)
            send[y] = jnp.where(first, odd, even)
        total = total + proto_term(dlog, emb[nodes, :])
    proto_out[...] = total


def pair_kernel(order, place, keep, other, *outs):
    for k, out in zip(order, outs):
        y = place[0] ^ k
        out[...] = keep[y] + other[y]


def last_kernel(*refs):
    *parts, out = refs
    total = parts[0][...]
    for part in parts[1:]:
        total = total + part[...]
    out[...] = jnp.transpose(total)


def call(kernel, name, outs, scratch, args, in_places=(), out_places=()):
    vmem = pl.BlockSpec(memory_space=pltpu.VMEM)
    place = lambda places, k: pl.BlockSpec(memory_space=places[k]) if k in places else vmem
    return pl.pallas_call(
        kernel,
        name=name,
        out_shape=[
            dict(out_places)[k](shape, dtype)
            if k in dict(out_places)
            else jax.ShapeDtypeStruct(shape, dtype)
            for k, (shape, dtype) in enumerate(outs)
        ],
        in_specs=[place(dict(in_places), k) for k in range(len(args))],
        out_specs=[place(dict(out_places), k) for k in range(len(outs))],
        scratch_shapes=[
            s if not isinstance(s, tuple) else pltpu.VMEM(s, F32) for s in scratch
        ],
        compiler_params=pltpu.CompilerParams(vmem_limit_bytes=24 * 2**20),
    )(*args)


def on_device(embeddings, prototypes, plan_grad):
    rows, width = embeddings.shape
    local = prototypes.shape[0]
    ys = lax.axis_size("y")
    comms = ys * lax.axis_size("core")
    xs = lax.axis_size("x")
    zs = lax.axis_size("z")
    per_proto = (rows * zs * xs) / (local * comms)
    log_mass = math.log2(per_proto)
    full = ((local, rows), F32)
    row = ((1, rows), F32)
    col = ((1, local), F32)
    two = ((2, local), F32)
    tall = (local, LANES)
    block = ((width, rows // comms), F32)
    blocks = ((ys,) + block[0], F32)
    node = ("z", "x")
    comm = ("y", "core")
    hbm = pltpu.HBM
    place = jnp.stack([lax.axis_index("y"), lax.axis_index("core")])

    logits, grads, here = call(
        scores_kernel, "scores", [full, ((local, rows), BF16), row],
        [(rows, width), (local, width), pltpu.VMEM((rows, local), BF16),
         pltpu.SemaphoreType.DMA((6,))],
        [pltpu.with_memory_space_constraint(x, hbm)
         for x in (embeddings, prototypes, plan_grad)],
        {0: hbm, 1: hbm, 2: hbm},
    )
    here, place = lax.optimization_barrier((here, place))
    f1, here = call(
        col_kernel, "col_lse", [row, col], [(8, rows), tall, tall], [logits, to_all(here, comm)]
    )
    g1, here = call(
        lambda *refs: row_kernel(log_mass, *refs), "row_lse", [col, row], [tall],
        [logits, to_all(here, node)],
    )
    f2, here = call(
        col_mean_kernel, "col_lse_mean", [row, two],
        [(16, rows), tall, tall, tall], [logits, to_all(here, comm), grads],
    )
    (here,) = call(merge_kernel, "merge_x", [two], [], [to_all(here, "x")])
    score, here = call(
        lambda *refs: df2_kernel(log_mass, *refs), "df2", [full, row], [tall, tall],
        [logits, f2, to_all(here, "z"), grads],
    )
    score, here = call(
        dg1_kernel, "dg1", [full, col], [(8, rows), (8, rows), tall, tall],
        [logits, f2, g1, to_all(here, comm), score],
    )
    score, here = call(
        lambda *refs: df1_kernel(log_mass, *refs), "df1", [full, row], [tall, tall],
        [logits, f1, g1, to_all(here, node), score],
    )
    keep, send, proto_part = call(
        grads_kernel, "grads", [blocks, blocks, ((local, width), F32)], [],
        [place, logits, f1, to_all(here, comm), score, embeddings, prototypes], {0: pltpu.SMEM},
    )
    other = lax.ppermute(send, "core", [(0, 1), (1, 0)])
    grad_proto = scatter_sum(proto_part.reshape(xs * zs, -1, width), node)
    order = (2, 1, 3, 0)
    parts = call(
        lambda *refs: pair_kernel(order, *refs), "emb_pair", [block] * ys, [],
        [place, keep, other], {0: pltpu.SMEM},
    )
    parts = [
        lax.ppermute(part, "y", [(y, y ^ k) for y in range(ys)]) if k else part
        for k, part in zip(order, parts)
    ]
    (grad_emb,) = call(last_kernel, "emb_last", [(block[0][::-1], F32)], [], parts)
    return grad_emb, grad_proto


def solution(mesh):
    split_mesh = Mesh(mesh.devices.reshape(4, 2, 16, 4), ("y", "core", "z", "x"))
    node = ("z", "x")
    comm = ("y", "core")
    in_specs = (P(node, None), P(comm, None), P(node, comm))
    out_specs = (P(node + comm, None), P(comm + node, None))
    return jax.shard_map(
        on_device, mesh=split_mesh, in_specs=in_specs, out_specs=out_specs, check_vma=False
    )
```

```python
import math

import jax
import jax.numpy as jnp
from jax import lax
from jax.experimental import pallas as pl
from jax.experimental.pallas import tpu as pltpu
from jax.sharding import Mesh
from jax.sharding import PartitionSpec as P

INV_EPS = 20.0
LOG2E = 1.0 / math.log(2.0)
LANES = 128
WIDE = 256
SPAN = 4
F32 = jnp.float32
BF16 = jnp.bfloat16
NT = (((1,), (1,)), ((), ()))
EVERY = slice(None)


def to_all(values, axis):
    count = lax.axis_size(axis)
    copies = jnp.broadcast_to(values[None], (count,) + values.shape)
    return lax.all_to_all(copies, axis, 0, 0, tiled=True)


def scatter_sum(blocks, axis):
    return jnp.sum(lax.all_to_all(blocks, axis, 0, 0, tiled=True), axis=0)


def split(x, pieces):
    out = []
    for _ in range(pieces):
        piece = x.astype(BF16)
        out.append(piece)
        x = x - piece.astype(F32)
    return out


def down(row):
    return jnp.transpose(jnp.broadcast_to(row, (LANES, row.shape[1])))


def tile_rows(at, tall):
    return pl.ds(pl.multiple_of(at * tall, tall), tall)


def lanes_of(ref, rows, tile):
    return ref[rows, tile * LANES : (tile + 1) * LANES]


def add_parts(parts):
    values = [parts[k] for k in range(parts.shape[0])]
    while len(values) > 1:
        values = [a + b for a, b in zip(values[::2], values[1::2])]
    return values[0]


def merge_parts(parts):
    count = parts.shape[0]
    peak = parts[0, 0:1, :]
    for k in range(1, count):
        peak = jnp.maximum(peak, parts[k, 0:1, :])
    mass = jnp.zeros(peak.shape, F32)
    mean = jnp.zeros(peak.shape, F32)
    for k in range(count):
        share = jnp.exp2(parts[k, 0:1, :] - peak)
        mass = mass + share
        if parts.shape[1] == 2:
            mean = mean + share * parts[k, 1:2, :]
    total = peak + jnp.log2(mass)
    return total if parts.shape[1] == 1 else (total, mean / mass)


def scores_kernel(
    emb, proto, grads,
    logits, turned, row_out, e_in, p_in, g_in, sems,
):
    chunks = 4
    size = emb.shape[0] // chunks
    get_p = pltpu.make_async_copy(proto, p_in, sems.at[0])
    get_p.start()
    get_e = []
    for k in range(chunks):
        rows = pl.ds(k * size, size)
        get_e.append(pltpu.make_async_copy(emb.at[rows], e_in.at[rows], sems.at[1 + k]))
        get_e[k].start()
    get_g = pltpu.make_async_copy(grads, g_in, sems.at[1 + chunks])
    get_g.start()
    get_p.wait()
    hi, mid, low = split(p_in[...] * (INV_EPS * LOG2E), 3)
    left = jnp.concatenate([hi, hi, hi, mid, mid, low], axis=1)
    for get in get_e:
        get.wait()
    for at in range(0, emb.shape[0], size):
        lanes = slice(at, at + size)
        hi, mid, low = split(e_in[lanes, :], 3)
        right = jnp.concatenate([hi, mid, low, hi, mid, hi], axis=1)
        tile = lax.dot_general(left, right, NT, preferred_element_type=F32)
        logits[:, lanes] = tile
        if at + size == emb.shape[0]:
            get_g.wait()
        peak = jnp.max(tile, axis=0, keepdims=True)
        mass = jnp.sum(jnp.exp2(tile - peak), axis=0, keepdims=True)
        row_out[:, lanes] = peak + jnp.log2(mass)
    eye = (
        lax.broadcasted_iota(jnp.int32, (WIDE, WIDE), 0)
        == lax.broadcasted_iota(jnp.int32, (WIDE, WIDE), 1)
    ).astype(F32).astype(BF16)
    for at in range(0, grads.shape[1], WIDE):
        turned[at : at + WIDE, :] = lax.dot_general(
            eye, g_in[:, at : at + WIDE], NT, preferred_element_type=F32
        ).astype(BF16)


def col_kernel(logits, parts, f1, lse_out, shifts, peaks, masses):
    tiles = logits.shape[1] // LANES
    count = logits.shape[0] // 8
    f1[...] = -merge_parts(parts)
    shifts[...] = jnp.broadcast_to(f1[...], shifts.shape)

    def step(at, _):
        rows = tile_rows(at, 8)
        moved = [lanes_of(logits, rows, k) + lanes_of(shifts, EVERY, k) for k in range(tiles)]
        peak = moved[0]
        for part in moved[1:]:
            peak = jnp.maximum(peak, part)
        mass = jnp.exp2(moved[0] - peak)
        for part in moved[1:]:
            mass = mass + jnp.exp2(part - peak)
        peaks[rows, :] = peak
        masses[rows, :] = mass
        return 0

    lax.fori_loop(0, count, step, 0, unroll=count)
    peak_t = jnp.transpose(peaks[...])
    peak = jnp.max(peak_t, axis=0, keepdims=True)
    mass = jnp.sum(jnp.transpose(masses[...]) * jnp.exp2(peak_t - peak), axis=0, keepdims=True)
    lse_out[...] = peak + jnp.log2(mass)


def merge_kernel(parts, out):
    total, mean = merge_parts(parts)
    out[0:1, :] = total
    out[1:2, :] = mean


def col_mean_kernel(logits, parts, grads, f2, out, shifts, peaks, masses, means):
    tiles = logits.shape[1] // LANES
    count = logits.shape[0] // 16
    f2[...] = -merge_parts(parts)
    shifts[...] = jnp.broadcast_to(f2[...], shifts.shape)

    def step(at, _):
        rows = tile_rows(at, 16)
        peak = lanes_of(logits, rows, 0) + lanes_of(shifts, EVERY, 0)
        for k in range(1, tiles):
            peak = jnp.maximum(peak, lanes_of(logits, rows, k) + lanes_of(shifts, EVERY, k))
        mass = jnp.zeros((16, LANES), F32)
        mean = jnp.zeros((16, LANES), F32)
        for k in range(tiles):
            term = jnp.exp2(lanes_of(logits, rows, k) + lanes_of(shifts, EVERY, k) - peak)
            mass = mass + term
            mean = mean + term * lanes_of(grads, rows, k).astype(F32)
        peaks[rows, :] = peak
        masses[rows, :] = mass
        means[rows, :] = mean
        return 0

    lax.fori_loop(0, count, step, 0, unroll=count)
    peak_t = jnp.transpose(peaks[...])
    peak = jnp.max(peak_t, axis=0, keepdims=True)
    share = jnp.exp2(peak_t - peak)
    mass = jnp.sum(jnp.transpose(masses[...]) * share, axis=0, keepdims=True)
    mean = jnp.sum(jnp.transpose(means[...]) * share, axis=0, keepdims=True)
    out[0:1, :] = peak + jnp.log2(mass)
    out[1:2, :] = mean / mass


def spans(ref, size):
    tiles = ref.shape[1] // LANES
    for at in range(0, tiles, size):
        yield [slice(k * LANES, (k + 1) * LANES) for k in range(at, at + size)]


def row_kernel(log_mass, logits, parts, g1, lse_out, shifts):
    g1[...] = log_mass - merge_parts(parts)
    shifts[...] = down(g1[...])
    count = logits.shape[0] // 8
    for lanes in spans(logits, SPAN):

        def highest(at, peak):
            rows = tile_rows(at, 8)
            move = shifts[rows, :]
            return [jnp.maximum(p, logits[rows, s] + move) for p, s in zip(peak, lanes)]

        peak = lax.fori_loop(
            0, count, highest, [jnp.full((8, LANES), -jnp.inf, F32)] * SPAN, unroll=count
        )
        peak = [jnp.max(part, axis=0, keepdims=True) for part in peak]

        def add(at, mass):
            rows = tile_rows(at, 8)
            move = shifts[rows, :]
            return [
                m + jnp.exp2(logits[rows, s] + move - p) for m, p, s in zip(mass, peak, lanes)
            ]

        mass = lax.fori_loop(0, count, add, [jnp.zeros((8, LANES), F32)] * SPAN, unroll=count)
        for p, m, s in zip(peak, mass, lanes):
            lse_out[:, s] = p + jnp.log2(jnp.sum(m, axis=0, keepdims=True))


def df2_kernel(log_mass, logits, f2, parts, grads, score, out, cols, weights):
    total, mean = merge_parts(parts)
    cols[...] = down(log_mass - total)
    weights[...] = down(mean)
    tall = 16
    count = logits.shape[0] // tall
    for lanes in spans(logits, SPAN):
        moves = [f2[:, s] for s in lanes]

        def add(at, total):
            rows = tile_rows(at, tall)
            move = cols[rows, :]
            weigh = weights[rows, :]
            new = []
            for t, m, s in zip(total, moves, lanes):
                term = jnp.exp2(logits[rows, s] + move + m)
                term = term * (grads[rows, s].astype(F32) - weigh)
                score[rows, s] = term
                new.append(t + term[:8] + term[8:])
            return new

        total = lax.fori_loop(0, count, add, [jnp.zeros((8, LANES), F32)] * SPAN, unroll=count)
        for t, s in zip(total, lanes):
            out[:, s] = jnp.sum(t, axis=0, keepdims=True)


def dg1_kernel(logits, f2, g1, parts, score, rest, out, rows_of, weights, cols, sums):
    tiles = logits.shape[1] // LANES
    count = logits.shape[0] // 8
    rows_of[...] = jnp.broadcast_to(f2[...], rows_of.shape)
    weights[...] = jnp.broadcast_to(add_parts(parts), weights.shape)
    cols[...] = down(g1[...])

    def step(at, _):
        rows = tile_rows(at, 8)
        move = cols[rows, :]
        total = jnp.zeros((8, LANES), F32)
        for k in range(tiles):
            term = jnp.exp2(lanes_of(logits, rows, k) + lanes_of(rows_of, EVERY, k) + move)
            term = term * lanes_of(weights, EVERY, k)
            rest[rows, k * LANES : (k + 1) * LANES] = lanes_of(score, rows, k) - term
            total = total + term
        sums[rows, :] = total
        return 0

    lax.fori_loop(0, count, step, 0, unroll=count)
    out[...] = -jnp.sum(jnp.transpose(sums[...]), axis=0, keepdims=True)


def df1_kernel(log_mass, logits, f1, g1, parts, score, rest, out, cols, weights):
    cols[...] = down(g1[...] - log_mass)
    weights[...] = down(add_parts(parts))
    count = logits.shape[0] // 8
    for lanes in spans(logits, SPAN):
        moves = [f1[:, s] for s in lanes]

        def add(at, total):
            rows = tile_rows(at, 8)
            move = cols[rows, :]
            weigh = weights[rows, :]
            new = []
            for t, m, s in zip(total, moves, lanes):
                term = jnp.exp2(logits[rows, s] + move + m) * weigh
                rest[rows, s] = score[rows, s] - term
                new.append(t + term)
            return new

        total = lax.fori_loop(0, count, add, [jnp.zeros((8, LANES), F32)] * SPAN, unroll=count)
        for t, s in zip(total, lanes):
            out[:, s] = -jnp.sum(t, axis=0, keepdims=True)


def grads_kernel(place, logits, f1, parts, score, emb, proto, keep, send, proto_out, total, sem):
    df1 = add_parts(parts)
    width = emb.shape[1]
    size = keep.shape[2]
    step = 4 * size
    pieces = []
    sums = jnp.zeros(total.shape, F32)
    for at in range(0, logits.shape[1], step):
        nodes = slice(at, at + step)
        dlog = score[:, nodes] - jnp.exp2(logits[:, nodes] + f1[:, nodes]) * df1[:, nodes]
        hi, low = split(dlog, 2)
        pieces.append((hi, low))
        e_hi, e_low = split(emb[nodes, :] * INV_EPS, 2)
        both = jnp.dot(hi, jnp.concatenate([e_hi, e_low], axis=1), preferred_element_type=F32)
        sums = sums + both[:, :width] + both[:, width:]
        sums = sums + jnp.dot(low, e_hi, preferred_element_type=F32)
    total[...] = sums
    write = pltpu.make_async_copy(total, proto_out, sem)
    write.start()
    p_hi, p_low = split(jnp.transpose(proto[...]) * INV_EPS, 2)
    p_both = jnp.concatenate([p_hi, p_low], axis=0)
    first = place[1] == 0
    for at, (hi, low) in enumerate(pieces):
        both = jnp.dot(p_both, hi, preferred_element_type=F32)
        part = both[:width] + both[width:] + jnp.dot(p_hi, low, preferred_element_type=F32)
        for k in range(0, step // size, 2):
            y = (at * (step // size) + k) // 2
            even = part[:, k * size : (k + 1) * size]
            odd = part[:, (k + 1) * size : (k + 2) * size]
            keep[y] = jnp.where(first, even, odd)
            send[y] = jnp.where(first, odd, even)
    write.wait()


def pair_kernel(order, place, keep, other, *outs):
    for k, out in zip(order, outs):
        y = place[0] ^ k
        out[...] = keep[y] + other[y]


def last_kernel(*refs):
    *parts, out = refs
    total = parts[0][...]
    for part in parts[1:]:
        total = total + part[...]
    out[...] = jnp.transpose(total)


def call(kernel, name, outs, scratch, args, in_places=(), out_places=()):
    vmem = pl.BlockSpec(memory_space=pltpu.VMEM)
    place = lambda places, k: pl.BlockSpec(memory_space=places[k]) if k in places else vmem
    return pl.pallas_call(
        kernel,
        name=name,
        out_shape=[
            dict(out_places)[k](shape, dtype)
            if k in dict(out_places)
            else jax.ShapeDtypeStruct(shape, dtype)
            for k, (shape, dtype) in enumerate(outs)
        ],
        in_specs=[place(dict(in_places), k) for k in range(len(args))],
        out_specs=[place(dict(out_places), k) for k in range(len(outs))],
        scratch_shapes=[
            s if not isinstance(s, tuple) else pltpu.VMEM(s, F32) for s in scratch
        ],
        compiler_params=pltpu.CompilerParams(vmem_limit_bytes=24 * 2**20),
    )(*args)


def on_device(embeddings, prototypes, plan_grad):
    rows, width = embeddings.shape
    local = prototypes.shape[0]
    ys = lax.axis_size("y")
    comms = ys * lax.axis_size("core")
    xs = lax.axis_size("x")
    zs = lax.axis_size("z")
    per_proto = (rows * zs * xs) / (local * comms)
    log_mass = math.log2(per_proto)
    full = ((local, rows), F32)
    row = ((1, rows), F32)
    col = ((1, local), F32)
    two = ((2, local), F32)
    tall = (local, LANES)
    block = ((width, rows // comms), F32)
    blocks = ((ys,) + block[0], F32)
    node = ("z", "x")
    comm = ("y", "core")
    hbm = pltpu.HBM
    place = jnp.stack([lax.axis_index("y"), lax.axis_index("core")])

    logits, grads, here = call(
        scores_kernel, "scores", [full, ((local, rows), BF16), row],
        [(rows, width), (local, width), pltpu.VMEM((rows, local), BF16),
         pltpu.SemaphoreType.DMA((6,))],
        [pltpu.with_memory_space_constraint(x, hbm)
         for x in (embeddings, prototypes, plan_grad)],
        {0: hbm, 1: hbm, 2: hbm},
    )
    here, place = lax.optimization_barrier((here, place))
    f1, here = call(
        col_kernel, "col_lse", [row, col], [(8, rows), tall, tall], [logits, to_all(here, comm)]
    )
    g1, here = call(
        lambda *refs: row_kernel(log_mass, *refs), "row_lse", [col, row], [tall],
        [logits, to_all(here, ("x", "z"))],
    )
    f2, here = call(
        col_mean_kernel, "col_lse_mean", [row, two],
        [(16, rows), tall, tall, tall], [logits, to_all(here, comm), grads],
    )
    (here,) = call(merge_kernel, "merge_x", [two], [], [to_all(here, "x")])
    score, here = call(
        lambda *refs: df2_kernel(log_mass, *refs), "df2", [full, row], [tall, tall],
        [logits, f2, to_all(here, "z"), grads],
    )
    score, here = call(
        dg1_kernel, "dg1", [full, col], [(8, rows), (8, rows), tall, tall],
        [logits, f2, g1, to_all(here, comm), score],
    )
    score, here = call(
        lambda *refs: df1_kernel(log_mass, *refs), "df1", [full, row], [tall, tall],
        [logits, f1, g1, to_all(here, ("x", "z")), score],
    )
    keep, send, proto_part = call(
        grads_kernel, "grads", [blocks, blocks, ((local, width), F32)],
        [(local, width), pltpu.SemaphoreType.DMA],
        [place, logits, f1, to_all(here, comm), score, embeddings, prototypes],
        {0: pltpu.SMEM}, {2: hbm},
    )
    other = lax.ppermute(send, "core", [(0, 1), (1, 0)])
    grad_proto = scatter_sum(proto_part.reshape(xs * zs, -1, width), node)
    order = (2, 1, 3, 0)
    parts = call(
        lambda *refs: pair_kernel(order, *refs), "emb_pair", [block] * ys, [],
        [place, keep, other], {0: pltpu.SMEM},
    )
    parts = [
        lax.ppermute(part, "y", [(y, y ^ k) for y in range(ys)]) if k else part
        for k, part in zip(order, parts)
    ]
    (grad_emb,) = call(last_kernel, "emb_last", [(block[0][::-1], F32)], [], parts)
    return grad_emb, grad_proto


def solution(mesh):
    split_mesh = Mesh(mesh.devices.reshape(4, 2, 16, 4), ("y", "core", "z", "x"))
    node = ("z", "x")
    comm = ("y", "core")
    in_specs = (P(node, None), P(comm, None), P(node, comm))
    out_specs = (P(node + comm, None), P(comm + node, None))
    return jax.shard_map(
        on_device, mesh=split_mesh, in_specs=in_specs, out_specs=out_specs, check_vma=False
    )
```

```python
import math

import jax
import jax.numpy as jnp
from jax import lax
from jax.experimental import pallas as pl
from jax.experimental.pallas import tpu as pltpu
from jax.sharding import Mesh
from jax.sharding import PartitionSpec as P

INV_EPS = 20.0
LOG2E = 1.0 / math.log(2.0)
LANES = 128
WIDE = 256
SPAN = 4
F32 = jnp.float32
BF16 = jnp.bfloat16
NT = (((1,), (1,)), ((), ()))
EVERY = slice(None)


def to_all(values, axis):
    count = lax.axis_size(axis)
    copies = jnp.broadcast_to(values[None], (count,) + values.shape)
    return lax.all_to_all(copies, axis, 0, 0, tiled=True)


def split(x, pieces):
    out = []
    for _ in range(pieces):
        piece = x.astype(BF16)
        out.append(piece)
        x = x - piece.astype(F32)
    return out


def down(row):
    return jnp.transpose(jnp.broadcast_to(row, (LANES, row.shape[1])))


def tile_rows(at, tall):
    return pl.ds(pl.multiple_of(at * tall, tall), tall)


def lanes_of(ref, rows, tile):
    return ref[rows, tile * LANES : (tile + 1) * LANES]


def add_parts(parts):
    values = [parts[k] for k in range(parts.shape[0])]
    while len(values) > 1:
        values = [a + b for a, b in zip(values[::2], values[1::2])]
    return values[0]


def merge_parts(parts):
    count = parts.shape[0]
    peak = parts[0, 0:1, :]
    for k in range(1, count):
        peak = jnp.maximum(peak, parts[k, 0:1, :])
    mass = jnp.zeros(peak.shape, F32)
    mean = jnp.zeros(peak.shape, F32)
    for k in range(count):
        share = jnp.exp2(parts[k, 0:1, :] - peak)
        mass = mass + share
        if parts.shape[1] == 2:
            mean = mean + share * parts[k, 1:2, :]
    total = peak + jnp.log2(mass)
    return total if parts.shape[1] == 1 else (total, mean / mass)


def scores_kernel(
    emb, proto, grads,
    logits, turned, row_out, e_in, p_in, g_in, sems,
):
    chunks = 4
    size = emb.shape[0] // chunks
    get_p = pltpu.make_async_copy(proto, p_in, sems.at[0])
    get_p.start()
    get_e = []
    for k in range(chunks):
        rows = pl.ds(k * size, size)
        get_e.append(pltpu.make_async_copy(emb.at[rows], e_in.at[rows], sems.at[1 + k]))
        get_e[k].start()
    get_g = pltpu.make_async_copy(grads, g_in, sems.at[1 + chunks])
    get_g.start()
    get_p.wait()
    hi, mid, low = split(p_in[...] * (INV_EPS * LOG2E), 3)
    left = jnp.concatenate([hi, hi, hi, mid, mid, low], axis=1)
    for get in get_e:
        get.wait()
    for at in range(0, emb.shape[0], size):
        lanes = slice(at, at + size)
        hi, mid, low = split(e_in[lanes, :], 3)
        right = jnp.concatenate([hi, mid, low, hi, mid, hi], axis=1)
        tile = lax.dot_general(left, right, NT, preferred_element_type=F32)
        logits[:, lanes] = tile
        if at + size == emb.shape[0]:
            get_g.wait()
        peak = jnp.max(tile, axis=0, keepdims=True)
        mass = jnp.sum(jnp.exp2(tile - peak), axis=0, keepdims=True)
        row_out[:, lanes] = peak + jnp.log2(mass)
    eye = (
        lax.broadcasted_iota(jnp.int32, (WIDE, WIDE), 0)
        == lax.broadcasted_iota(jnp.int32, (WIDE, WIDE), 1)
    ).astype(F32).astype(BF16)
    for at in range(0, grads.shape[1], WIDE):
        turned[at : at + WIDE, :] = lax.dot_general(
            eye, g_in[:, at : at + WIDE], NT, preferred_element_type=F32
        ).astype(BF16)


def col_kernel(logits, parts, f1, lse_out, shifts, peaks, masses):
    tiles = logits.shape[1] // LANES
    count = logits.shape[0] // 8
    f1[...] = -merge_parts(parts)
    shifts[...] = jnp.broadcast_to(f1[...], shifts.shape)

    def step(at, _):
        rows = tile_rows(at, 8)
        moved = [lanes_of(logits, rows, k) + lanes_of(shifts, EVERY, k) for k in range(tiles)]
        peak = moved[0]
        for part in moved[1:]:
            peak = jnp.maximum(peak, part)
        mass = jnp.exp2(moved[0] - peak)
        for part in moved[1:]:
            mass = mass + jnp.exp2(part - peak)
        peaks[rows, :] = peak
        masses[rows, :] = mass
        return 0

    lax.fori_loop(0, count, step, 0, unroll=count)
    peak_t = jnp.transpose(peaks[...])
    peak = jnp.max(peak_t, axis=0, keepdims=True)
    mass = jnp.sum(jnp.transpose(masses[...]) * jnp.exp2(peak_t - peak), axis=0, keepdims=True)
    lse_out[...] = peak + jnp.log2(mass)


def merge_kernel(parts, out):
    total, mean = merge_parts(parts)
    out[0:1, :] = total
    out[1:2, :] = mean


def col_mean_kernel(logits, parts, grads, f2, out, shifts, peaks, masses, means):
    tiles = logits.shape[1] // LANES
    count = logits.shape[0] // 16
    f2[...] = -merge_parts(parts)
    shifts[...] = jnp.broadcast_to(f2[...], shifts.shape)

    def step(at, _):
        rows = tile_rows(at, 16)
        peak = lanes_of(logits, rows, 0) + lanes_of(shifts, EVERY, 0)
        for k in range(1, tiles):
            peak = jnp.maximum(peak, lanes_of(logits, rows, k) + lanes_of(shifts, EVERY, k))
        mass = jnp.zeros((16, LANES), F32)
        mean = jnp.zeros((16, LANES), F32)
        for k in range(tiles):
            term = jnp.exp2(lanes_of(logits, rows, k) + lanes_of(shifts, EVERY, k) - peak)
            mass = mass + term
            mean = mean + term * lanes_of(grads, rows, k).astype(F32)
        peaks[rows, :] = peak
        masses[rows, :] = mass
        means[rows, :] = mean
        return 0

    lax.fori_loop(0, count, step, 0, unroll=count)
    peak_t = jnp.transpose(peaks[...])
    peak = jnp.max(peak_t, axis=0, keepdims=True)
    share = jnp.exp2(peak_t - peak)
    mass = jnp.sum(jnp.transpose(masses[...]) * share, axis=0, keepdims=True)
    mean = jnp.sum(jnp.transpose(means[...]) * share, axis=0, keepdims=True)
    out[0:1, :] = peak + jnp.log2(mass)
    out[1:2, :] = mean / mass


def spans(ref, size):
    tiles = ref.shape[1] // LANES
    for at in range(0, tiles, size):
        yield [slice(k * LANES, (k + 1) * LANES) for k in range(at, at + size)]


def row_kernel(log_mass, logits, parts, g1, lse_out, shifts):
    g1[...] = log_mass - merge_parts(parts)
    shifts[...] = down(g1[...])
    count = logits.shape[0] // 8
    for lanes in spans(logits, SPAN):

        def highest(at, peak):
            rows = tile_rows(at, 8)
            move = shifts[rows, :]
            return [jnp.maximum(p, logits[rows, s] + move) for p, s in zip(peak, lanes)]

        peak = lax.fori_loop(
            0, count, highest, [jnp.full((8, LANES), -jnp.inf, F32)] * SPAN, unroll=count
        )
        peak = [jnp.max(part, axis=0, keepdims=True) for part in peak]

        def add(at, mass):
            rows = tile_rows(at, 8)
            move = shifts[rows, :]
            return [
                m + jnp.exp2(logits[rows, s] + move - p) for m, p, s in zip(mass, peak, lanes)
            ]

        mass = lax.fori_loop(0, count, add, [jnp.zeros((8, LANES), F32)] * SPAN, unroll=count)
        for p, m, s in zip(peak, mass, lanes):
            lse_out[:, s] = p + jnp.log2(jnp.sum(m, axis=0, keepdims=True))


def df2_kernel(log_mass, logits, f2, parts, grads, score, out, cols, weights):
    total, mean = merge_parts(parts)
    cols[...] = down(log_mass - total)
    weights[...] = down(mean)
    tall = 16
    count = logits.shape[0] // tall
    for lanes in spans(logits, SPAN):
        moves = [f2[:, s] for s in lanes]

        def add(at, total):
            rows = tile_rows(at, tall)
            move = cols[rows, :]
            weigh = weights[rows, :]
            new = []
            for t, m, s in zip(total, moves, lanes):
                term = jnp.exp2(logits[rows, s] + move + m)
                term = term * (grads[rows, s].astype(F32) - weigh)
                score[rows, s] = term
                new.append(t + term[:8] + term[8:])
            return new

        total = lax.fori_loop(0, count, add, [jnp.zeros((8, LANES), F32)] * SPAN, unroll=count)
        for t, s in zip(total, lanes):
            out[:, s] = jnp.sum(t, axis=0, keepdims=True)


def dg1_kernel(logits, f2, g1, parts, score, rest, out, rows_of, weights, cols, sums):
    tiles = logits.shape[1] // LANES
    count = logits.shape[0] // 8
    rows_of[...] = jnp.broadcast_to(f2[...], rows_of.shape)
    weights[...] = jnp.broadcast_to(add_parts(parts), weights.shape)
    cols[...] = down(g1[...])

    def step(at, _):
        rows = tile_rows(at, 8)
        move = cols[rows, :]
        total = jnp.zeros((8, LANES), F32)
        for k in range(tiles):
            term = jnp.exp2(lanes_of(logits, rows, k) + lanes_of(rows_of, EVERY, k) + move)
            term = term * lanes_of(weights, EVERY, k)
            rest[rows, k * LANES : (k + 1) * LANES] = lanes_of(score, rows, k) - term
            total = total + term
        sums[rows, :] = total
        return 0

    lax.fori_loop(0, count, step, 0, unroll=count)
    out[...] = -jnp.sum(jnp.transpose(sums[...]), axis=0, keepdims=True)


def df1_kernel(log_mass, logits, f1, g1, parts, score, rest, out, cols, weights):
    cols[...] = down(g1[...] - log_mass)
    weights[...] = down(add_parts(parts))
    count = logits.shape[0] // 8
    for lanes in spans(logits, SPAN):
        moves = [f1[:, s] for s in lanes]

        def add(at, total):
            rows = tile_rows(at, 8)
            move = cols[rows, :]
            weigh = weights[rows, :]
            new = []
            for t, m, s in zip(total, moves, lanes):
                term = jnp.exp2(logits[rows, s] + move + m) * weigh
                rest[rows, s] = score[rows, s] - term
                new.append(t + term)
            return new

        total = lax.fori_loop(0, count, add, [jnp.zeros((8, LANES), F32)] * SPAN, unroll=count)
        for t, s in zip(total, lanes):
            out[:, s] = -jnp.sum(t, axis=0, keepdims=True)


def grads_kernel(place, logits, f1, parts, score, emb, proto, keep, send, proto_out, total, sem):
    df1 = add_parts(parts)
    width = emb.shape[1]
    size = keep.shape[2]
    step = 4 * size
    pieces = []
    sums = jnp.zeros((logits.shape[0], width), F32)
    for at in range(0, logits.shape[1], step):
        nodes = slice(at, at + step)
        dlog = score[:, nodes] - jnp.exp2(logits[:, nodes] + f1[:, nodes]) * df1[:, nodes]
        hi, low = split(dlog, 2)
        pieces.append((hi, low))
        e_hi, e_low = split(emb[nodes, :] * INV_EPS, 2)
        both = jnp.dot(hi, jnp.concatenate([e_hi, e_low], axis=1), preferred_element_type=F32)
        sums = sums + both[:, :width] + both[:, width:]
        sums = sums + jnp.dot(low, e_hi, preferred_element_type=F32)
    xs, zs, tall, _ = total.shape
    for x in range(xs):
        for z in range(zs):
            start = (z * xs + x) * tall
            total[x, z] = sums[start : start + tall]
    write = pltpu.make_async_copy(total, proto_out, sem)
    write.start()
    p_hi, p_low = split(jnp.transpose(proto[...]) * INV_EPS, 2)
    p_both = jnp.concatenate([p_hi, p_low], axis=0)
    first = place[1] == 0
    for at, (hi, low) in enumerate(pieces):
        both = jnp.dot(p_both, hi, preferred_element_type=F32)
        part = both[:width] + both[width:] + jnp.dot(p_hi, low, preferred_element_type=F32)
        for k in range(0, step // size, 2):
            y = (at * (step // size) + k) // 2
            even = part[:, k * size : (k + 1) * size]
            odd = part[:, (k + 1) * size : (k + 2) * size]
            keep[y] = jnp.where(first, even, odd)
            send[y] = jnp.where(first, odd, even)
    write.wait()


def pair_kernel(order, place, keep, other, *outs):
    for k, out in zip(order, outs):
        y = place[0] ^ k
        out[...] = keep[y] + other[y]


def last_kernel(far, near, next_to, own, blocks, emb_out, proto_out):
    emb_out[...] = jnp.transpose((far[...] + near[...]) + (next_to[...] + own[...]))
    proto_out[...] = add_parts(blocks)


def call(kernel, name, outs, scratch, args, in_places=(), out_places=()):
    vmem = pl.BlockSpec(memory_space=pltpu.VMEM)
    place = lambda places, k: pl.BlockSpec(memory_space=places[k]) if k in places else vmem
    return pl.pallas_call(
        kernel,
        name=name,
        out_shape=[
            dict(out_places)[k](shape, dtype)
            if k in dict(out_places)
            else jax.ShapeDtypeStruct(shape, dtype)
            for k, (shape, dtype) in enumerate(outs)
        ],
        in_specs=[place(dict(in_places), k) for k in range(len(args))],
        out_specs=[place(dict(out_places), k) for k in range(len(outs))],
        scratch_shapes=[
            s if not isinstance(s, tuple) else pltpu.VMEM(s, F32) for s in scratch
        ],
        compiler_params=pltpu.CompilerParams(vmem_limit_bytes=24 * 2**20),
    )(*args)


def on_device(embeddings, prototypes, plan_grad):
    rows, width = embeddings.shape
    local = prototypes.shape[0]
    ys = lax.axis_size("y")
    comms = ys * lax.axis_size("core")
    xs = lax.axis_size("x")
    zs = lax.axis_size("z")
    per_proto = (rows * zs * xs) / (local * comms)
    log_mass = math.log2(per_proto)
    full = ((local, rows), F32)
    row = ((1, rows), F32)
    col = ((1, local), F32)
    two = ((2, local), F32)
    tall = (local, LANES)
    block = ((width, rows // comms), F32)
    blocks = ((ys,) + block[0], F32)
    node = ("z", "x")
    comm = ("y", "core")
    by_node = ((xs, zs, local // (xs * zs), width), F32)
    hbm = pltpu.HBM
    place = jnp.stack([lax.axis_index("y"), lax.axis_index("core")])

    logits, grads, here = call(
        scores_kernel, "scores", [full, ((local, rows), BF16), row],
        [(rows, width), (local, width), pltpu.VMEM((rows, local), BF16),
         pltpu.SemaphoreType.DMA((6,))],
        [pltpu.with_memory_space_constraint(x, hbm)
         for x in (embeddings, prototypes, plan_grad)],
        {0: hbm, 1: hbm, 2: hbm},
    )
    here, place = lax.optimization_barrier((here, place))
    f1, here = call(
        col_kernel, "col_lse", [row, col], [(8, rows), tall, tall], [logits, to_all(here, comm)]
    )
    g1, here = call(
        lambda *refs: row_kernel(log_mass, *refs), "row_lse", [col, row], [tall],
        [logits, to_all(here, ("x", "z"))],
    )
    f2, here = call(
        col_mean_kernel, "col_lse_mean", [row, two],
        [(16, rows), tall, tall, tall], [logits, to_all(here, comm), grads],
    )
    (here,) = call(merge_kernel, "merge_x", [two], [], [to_all(here, "x")])
    score, here = call(
        lambda *refs: df2_kernel(log_mass, *refs), "df2", [full, row], [tall, tall],
        [logits, f2, to_all(here, "z"), grads],
    )
    score, here = call(
        dg1_kernel, "dg1", [full, col], [(8, rows), (8, rows), tall, tall],
        [logits, f2, g1, to_all(here, comm), score],
    )
    score, here = call(
        lambda *refs: df1_kernel(log_mass, *refs), "df1", [full, row], [tall, tall],
        [logits, f1, g1, to_all(here, ("x", "z")), score],
    )
    keep, send, proto_part = call(
        grads_kernel, "grads", [blocks, blocks, by_node],
        [by_node[0], pltpu.SemaphoreType.DMA],
        [place, logits, f1, to_all(here, comm), score, embeddings, prototypes],
        {0: pltpu.SMEM}, {2: hbm},
    )
    other = lax.ppermute(send, "core", [(0, 1), (1, 0)])
    proto_part = proto_part.reshape(xs * zs, -1, width)
    proto_part = lax.all_to_all(proto_part, ("x", "z"), 0, 0, tiled=True)
    order = (2, 1, 3, 0)
    parts = call(
        lambda *refs: pair_kernel(order, *refs), "emb_pair", [block] * ys, [],
        [place, keep, other], {0: pltpu.SMEM},
    )
    parts = [
        lax.ppermute(part, "y", [(y, y ^ k) for y in range(ys)]) if k else part
        for k, part in zip(order, parts)
    ]
    grad_emb, grad_proto = call(
        last_kernel, "last", [(block[0][::-1], F32), (proto_part.shape[1:], F32)], [],
        parts + [proto_part],
    )
    return grad_emb, grad_proto


def solution(mesh):
    split_mesh = Mesh(mesh.devices.reshape(4, 2, 16, 4), ("y", "core", "z", "x"))
    node = ("z", "x")
    comm = ("y", "core")
    in_specs = (P(node, None), P(comm, None), P(node, comm))
    out_specs = (P(node + comm, None), P(comm + node, None))
    return jax.shard_map(
        on_device, mesh=split_mesh, in_specs=in_specs, out_specs=out_specs, check_vma=False
    )
```

```python
import math

import jax
import jax.numpy as jnp
from jax import lax
from jax.experimental import pallas as pl
from jax.experimental.pallas import tpu as pltpu
from jax.sharding import Mesh
from jax.sharding import PartitionSpec as P

INV_EPS = 20.0
LOG2E = 1.0 / math.log(2.0)
LANES = 128
WIDE = 256
SPAN = 4
F32 = jnp.float32
BF16 = jnp.bfloat16
NT = (((1,), (1,)), ((), ()))
EVERY = slice(None)


def to_all(values, axis):
    count = lax.axis_size(axis)
    copies = jnp.broadcast_to(values[None], (count,) + values.shape)
    return lax.all_to_all(copies, axis, 0, 0, tiled=True)


def split(x, pieces):
    out = []
    for _ in range(pieces):
        piece = x.astype(BF16)
        out.append(piece)
        x = x - piece.astype(F32)
    return out


def down(row):
    return jnp.transpose(jnp.broadcast_to(row, (LANES, row.shape[1])))


def tile_rows(at, tall):
    return pl.ds(pl.multiple_of(at * tall, tall), tall)


def lanes_of(ref, rows, tile):
    return ref[rows, tile * LANES : (tile + 1) * LANES]


def add_parts(parts):
    values = [parts[k] for k in range(parts.shape[0])]
    while len(values) > 1:
        values = [a + b for a, b in zip(values[::2], values[1::2])]
    return values[0]


def merge_parts(parts):
    count = parts.shape[0]
    peak = parts[0, 0:1, :]
    for k in range(1, count):
        peak = jnp.maximum(peak, parts[k, 0:1, :])
    mass = jnp.zeros(peak.shape, F32)
    mean = jnp.zeros(peak.shape, F32)
    for k in range(count):
        share = jnp.exp2(parts[k, 0:1, :] - peak)
        mass = mass + share
        if parts.shape[1] == 2:
            mean = mean + share * parts[k, 1:2, :]
    total = peak + jnp.log2(mass)
    return total if parts.shape[1] == 1 else (total, mean / mass)


def scores_kernel(
    emb, proto, grads,
    logits, turned, row_out, e_in, p_in, g_in, sems,
):
    chunks = 4
    size = emb.shape[0] // chunks
    get_p = pltpu.make_async_copy(proto, p_in, sems.at[0])
    get_p.start()
    get_e = []
    for k in range(chunks):
        rows = pl.ds(k * size, size)
        get_e.append(pltpu.make_async_copy(emb.at[rows], e_in.at[rows], sems.at[1 + k]))
        get_e[k].start()
    get_g = pltpu.make_async_copy(grads, g_in, sems.at[1 + chunks])
    get_g.start()
    get_p.wait()
    hi, mid, low = split(p_in[...] * (INV_EPS * LOG2E), 3)
    left = jnp.concatenate([hi, hi, hi, mid, mid, low], axis=1)
    for get in get_e:
        get.wait()
    for at in range(0, emb.shape[0], size):
        lanes = slice(at, at + size)
        hi, mid, low = split(e_in[lanes, :], 3)
        right = jnp.concatenate([hi, mid, low, hi, mid, hi], axis=1)
        tile = lax.dot_general(left, right, NT, preferred_element_type=F32)
        logits[:, lanes] = tile
        if at + size == emb.shape[0]:
            get_g.wait()
        peak = jnp.max(tile, axis=0, keepdims=True)
        mass = jnp.sum(jnp.exp2(tile - peak), axis=0, keepdims=True)
        row_out[:, lanes] = peak + jnp.log2(mass)
    eye = (
        lax.broadcasted_iota(jnp.int32, (WIDE, WIDE), 0)
        == lax.broadcasted_iota(jnp.int32, (WIDE, WIDE), 1)
    ).astype(F32).astype(BF16)
    for at in range(0, grads.shape[1], WIDE):
        turned[at : at + WIDE, :] = lax.dot_general(
            eye, g_in[:, at : at + WIDE], NT, preferred_element_type=F32
        ).astype(BF16)


def col_kernel(logits, parts, f1, lse_out, shifts, peaks, masses):
    tiles = logits.shape[1] // LANES
    count = logits.shape[0] // 8
    f1[...] = -merge_parts(parts)
    shifts[...] = jnp.broadcast_to(f1[...], shifts.shape)

    def step(at, _):
        rows = tile_rows(at, 8)
        moved = [lanes_of(logits, rows, k) + lanes_of(shifts, EVERY, k) for k in range(tiles)]
        peak = moved[0]
        for part in moved[1:]:
            peak = jnp.maximum(peak, part)
        mass = jnp.exp2(moved[0] - peak)
        for part in moved[1:]:
            mass = mass + jnp.exp2(part - peak)
        peaks[rows, :] = peak
        masses[rows, :] = mass
        return 0

    lax.fori_loop(0, count, step, 0, unroll=count)
    peak_t = jnp.transpose(peaks[...])
    peak = jnp.max(peak_t, axis=0, keepdims=True)
    mass = jnp.sum(jnp.transpose(masses[...]) * jnp.exp2(peak_t - peak), axis=0, keepdims=True)
    lse_out[...] = peak + jnp.log2(mass)


def merge_kernel(parts, out):
    total, mean = merge_parts(parts)
    out[0:1, :] = total
    out[1:2, :] = mean


def col_mean_kernel(logits, parts, grads, f2, out, shifts, peaks, masses, means):
    tiles = logits.shape[1] // LANES
    count = logits.shape[0] // 16
    f2[...] = -merge_parts(parts)
    shifts[...] = jnp.broadcast_to(f2[...], shifts.shape)

    def step(at, _):
        rows = tile_rows(at, 16)
        peak = lanes_of(logits, rows, 0) + lanes_of(shifts, EVERY, 0)
        for k in range(1, tiles):
            peak = jnp.maximum(peak, lanes_of(logits, rows, k) + lanes_of(shifts, EVERY, k))
        mass = jnp.zeros((16, LANES), F32)
        mean = jnp.zeros((16, LANES), F32)
        for k in range(tiles):
            term = jnp.exp2(lanes_of(logits, rows, k) + lanes_of(shifts, EVERY, k) - peak)
            mass = mass + term
            mean = mean + term * lanes_of(grads, rows, k).astype(F32)
        peaks[rows, :] = peak
        masses[rows, :] = mass
        means[rows, :] = mean
        return 0

    lax.fori_loop(0, count, step, 0, unroll=count)
    peak_t = jnp.transpose(peaks[...])
    peak = jnp.max(peak_t, axis=0, keepdims=True)
    share = jnp.exp2(peak_t - peak)
    mass = jnp.sum(jnp.transpose(masses[...]) * share, axis=0, keepdims=True)
    mean = jnp.sum(jnp.transpose(means[...]) * share, axis=0, keepdims=True)
    out[0:1, :] = peak + jnp.log2(mass)
    out[1:2, :] = mean / mass


def spans(ref, size):
    tiles = ref.shape[1] // LANES
    for at in range(0, tiles, size):
        yield [slice(k * LANES, (k + 1) * LANES) for k in range(at, at + size)]


def row_kernel(log_mass, logits, parts, g1, lse_out, shifts):
    g1[...] = log_mass - merge_parts(parts)
    shifts[...] = down(g1[...])
    count = logits.shape[0] // 8
    for lanes in spans(logits, SPAN):

        def highest(at, peak):
            rows = tile_rows(at, 8)
            move = shifts[rows, :]
            return [jnp.maximum(p, logits[rows, s] + move) for p, s in zip(peak, lanes)]

        peak = lax.fori_loop(
            0, count, highest, [jnp.full((8, LANES), -jnp.inf, F32)] * SPAN, unroll=count
        )
        peak = [jnp.max(part, axis=0, keepdims=True) for part in peak]

        def add(at, mass):
            rows = tile_rows(at, 8)
            move = shifts[rows, :]
            return [
                m + jnp.exp2(logits[rows, s] + move - p) for m, p, s in zip(mass, peak, lanes)
            ]

        mass = lax.fori_loop(0, count, add, [jnp.zeros((8, LANES), F32)] * SPAN, unroll=count)
        for p, m, s in zip(peak, mass, lanes):
            lse_out[:, s] = p + jnp.log2(jnp.sum(m, axis=0, keepdims=True))


def df2_kernel(log_mass, logits, f2, parts, grads, score, out, cols, weights):
    total, mean = merge_parts(parts)
    cols[...] = down(log_mass - total)
    weights[...] = down(mean)
    tall = 16
    count = logits.shape[0] // tall
    for lanes in spans(logits, SPAN):
        moves = [f2[:, s] for s in lanes]

        def add(at, total):
            rows = tile_rows(at, tall)
            move = cols[rows, :]
            weigh = weights[rows, :]
            new = []
            for t, m, s in zip(total, moves, lanes):
                term = jnp.exp2(logits[rows, s] + move + m)
                term = term * (grads[rows, s].astype(F32) - weigh)
                score[rows, s] = term
                new.append(t + term[:8] + term[8:])
            return new

        total = lax.fori_loop(0, count, add, [jnp.zeros((8, LANES), F32)] * SPAN, unroll=count)
        for t, s in zip(total, lanes):
            out[:, s] = jnp.sum(t, axis=0, keepdims=True)


def dg1_kernel(logits, f2, g1, parts, score, rest, out, rows_of, weights, cols, sums):
    tiles = logits.shape[1] // LANES
    count = logits.shape[0] // 8
    rows_of[...] = jnp.broadcast_to(f2[...], rows_of.shape)
    weights[...] = jnp.broadcast_to(add_parts(parts), weights.shape)
    cols[...] = down(g1[...])

    def step(at, _):
        rows = tile_rows(at, 8)
        move = cols[rows, :]
        total = jnp.zeros((8, LANES), F32)
        for k in range(tiles):
            term = jnp.exp2(lanes_of(logits, rows, k) + lanes_of(rows_of, EVERY, k) + move)
            term = term * lanes_of(weights, EVERY, k)
            rest[rows, k * LANES : (k + 1) * LANES] = lanes_of(score, rows, k) - term
            total = total + term
        sums[rows, :] = total
        return 0

    lax.fori_loop(0, count, step, 0, unroll=count)
    out[...] = -jnp.sum(jnp.transpose(sums[...]), axis=0, keepdims=True)


def df1_kernel(log_mass, logits, f1, g1, parts, score, rest, out, cols, weights):
    cols[...] = down(g1[...] - log_mass)
    weights[...] = down(add_parts(parts))
    count = logits.shape[0] // 8
    for lanes in spans(logits, SPAN):
        moves = [f1[:, s] for s in lanes]

        def add(at, total):
            rows = tile_rows(at, 8)
            move = cols[rows, :]
            weigh = weights[rows, :]
            new = []
            for t, m, s in zip(total, moves, lanes):
                term = jnp.exp2(logits[rows, s] + move + m) * weigh
                rest[rows, s] = score[rows, s] - term
                new.append(t + term)
            return new

        total = lax.fori_loop(0, count, add, [jnp.zeros((8, LANES), F32)] * SPAN, unroll=count)
        for t, s in zip(total, lanes):
            out[:, s] = -jnp.sum(t, axis=0, keepdims=True)


def grads_kernel(place, logits, f1, parts, score, emb, proto, keep, send, proto_out, total, sem):
    df1 = add_parts(parts)
    width = emb.shape[1]
    size = keep.shape[2]
    step = 4 * size
    pieces = []
    sums = jnp.zeros((logits.shape[0], width), F32)
    for at in range(0, logits.shape[1], step):
        nodes = slice(at, at + step)
        dlog = score[:, nodes] - jnp.exp2(logits[:, nodes] + f1[:, nodes]) * df1[:, nodes]
        hi, low = split(dlog, 2)
        pieces.append((hi, low))
        e_hi, e_low = split(emb[nodes, :] * INV_EPS, 2)
        both = jnp.dot(hi, jnp.concatenate([e_hi, e_low], axis=1), preferred_element_type=F32)
        sums = sums + both[:, :width] + both[:, width:]
        sums = sums + jnp.dot(low, e_hi, preferred_element_type=F32)
    xs, zs, tall, _ = total.shape
    for x in range(xs):
        for z in range(zs):
            start = (z * xs + x) * tall
            total[x, z] = sums[start : start + tall]
    write = pltpu.make_async_copy(total, proto_out, sem)
    write.start()
    p_hi, p_low = split(jnp.transpose(proto[...]) * INV_EPS, 2)
    p_both = jnp.concatenate([p_hi, p_low], axis=0)
    first = place[1] == 0
    for at, (hi, low) in enumerate(pieces):
        both = jnp.dot(p_both, hi, preferred_element_type=F32)
        part = both[:width] + both[width:] + jnp.dot(p_hi, low, preferred_element_type=F32)
        for k in range(0, step // size, 2):
            y = (at * (step // size) + k) // 2
            even = part[:, k * size : (k + 1) * size]
            odd = part[:, (k + 1) * size : (k + 2) * size]
            keep[y] = jnp.where(first, even, odd)
            send[y] = jnp.where(first, odd, even)
    write.wait()


def pair_kernel(order, place, keep, other, *outs):
    for k, out in zip(order, outs):
        y = place[0] ^ k
        out[...] = keep[y] + other[y]


def last_kernel(far, near, next_to, own, blocks, emb_out, proto_out):
    emb_out[...] = jnp.transpose((far[...] + near[...]) + (next_to[...] + own[...]))
    proto_out[...] = add_parts(blocks)


def call(kernel, name, outs, scratch, args, in_places=(), out_places=()):
    vmem = pl.BlockSpec(memory_space=pltpu.VMEM)
    place = lambda places, k: pl.BlockSpec(memory_space=places[k]) if k in places else vmem
    return pl.pallas_call(
        kernel,
        name=name,
        out_shape=[
            dict(out_places)[k](shape, dtype)
            if k in dict(out_places)
            else jax.ShapeDtypeStruct(shape, dtype)
            for k, (shape, dtype) in enumerate(outs)
        ],
        in_specs=[place(dict(in_places), k) for k in range(len(args))],
        out_specs=[place(dict(out_places), k) for k in range(len(outs))],
        scratch_shapes=[
            s if not isinstance(s, tuple) else pltpu.VMEM(s, F32) for s in scratch
        ],
        compiler_params=pltpu.CompilerParams(vmem_limit_bytes=24 * 2**20),
    )(*args)


def on_device(embeddings, prototypes, plan_grad):
    rows, width = embeddings.shape
    local = prototypes.shape[0]
    ys = lax.axis_size("y")
    comms = ys * lax.axis_size("core")
    xs = lax.axis_size("x")
    zs = lax.axis_size("z")
    per_proto = (rows * zs * xs) / (local * comms)
    log_mass = math.log2(per_proto)
    full = ((local, rows), F32)
    row = ((1, rows), F32)
    col = ((1, local), F32)
    two = ((2, local), F32)
    tall = (local, LANES)
    block = ((width, rows // comms), F32)
    blocks = ((ys,) + block[0], F32)
    node = ("z", "x")
    comm = ("y", "core")
    by_node = ((xs, zs, local // (xs * zs), width), F32)
    hbm = pltpu.HBM
    place = jnp.stack([lax.axis_index("y"), lax.axis_index("core")])

    logits, grads, here = call(
        scores_kernel, "scores", [full, ((local, rows), BF16), row],
        [(rows, width), (local, width), pltpu.VMEM((rows, local), BF16),
         pltpu.SemaphoreType.DMA((6,))],
        [pltpu.with_memory_space_constraint(x, hbm)
         for x in (embeddings, prototypes, plan_grad)],
        {0: hbm, 1: hbm, 2: hbm},
    )
    here, place = lax.optimization_barrier((here, place))
    f1, here = call(
        col_kernel, "col_lse", [row, col], [(8, rows), tall, tall], [logits, to_all(here, ("core", "y"))]
    )
    g1, here = call(
        lambda *refs: row_kernel(log_mass, *refs), "row_lse", [col, row], [tall],
        [logits, to_all(here, ("x", "z"))],
    )
    f2, here = call(
        col_mean_kernel, "col_lse_mean", [row, two],
        [(16, rows), tall, tall, tall], [logits, to_all(here, ("core", "y")), grads],
    )
    (here,) = call(merge_kernel, "merge_x", [two], [], [to_all(here, "x")])
    score, here = call(
        lambda *refs: df2_kernel(log_mass, *refs), "df2", [full, row], [tall, tall],
        [logits, f2, to_all(here, "z"), grads],
    )
    score, here = call(
        dg1_kernel, "dg1", [full, col], [(8, rows), (8, rows), tall, tall],
        [logits, f2, g1, to_all(here, ("core", "y")), score],
    )
    score, here = call(
        lambda *refs: df1_kernel(log_mass, *refs), "df1", [full, row], [tall, tall],
        [logits, f1, g1, to_all(here, ("x", "z")), score],
    )
    keep, send, proto_part = call(
        grads_kernel, "grads", [blocks, blocks, by_node],
        [by_node[0], pltpu.SemaphoreType.DMA],
        [place, logits, f1, to_all(here, ("core", "y")), score, embeddings, prototypes],
        {0: pltpu.SMEM}, {2: hbm},
    )
    other = lax.ppermute(send, "core", [(0, 1), (1, 0)])
    proto_part = proto_part.reshape(xs * zs, -1, width)
    proto_part = lax.all_to_all(proto_part, ("x", "z"), 0, 0, tiled=True)
    order = (2, 1, 3, 0)
    parts = call(
        lambda *refs: pair_kernel(order, *refs), "emb_pair", [block] * ys, [],
        [place, keep, other], {0: pltpu.SMEM},
    )
    parts = [
        lax.ppermute(part, "y", [(y, y ^ k) for y in range(ys)]) if k else part
        for k, part in zip(order, parts)
    ]
    grad_emb, grad_proto = call(
        last_kernel, "last", [(block[0][::-1], F32), (proto_part.shape[1:], F32)], [],
        parts + [proto_part],
    )
    return grad_emb, grad_proto


def solution(mesh):
    split_mesh = Mesh(mesh.devices.reshape(4, 2, 16, 4), ("y", "core", "z", "x"))
    node = ("z", "x")
    comm = ("y", "core")
    in_specs = (P(node, None), P(comm, None), P(node, comm))
    out_specs = (P(node + comm, None), P(comm + node, None))
    return jax.shard_map(
        on_device, mesh=split_mesh, in_specs=in_specs, out_specs=out_specs, check_vma=False
    )
```
